256 devices in a mesh: lat: 8 (over y_hi, x), lon: 32 (over y_lo, z, core).
Axes of the slice: x: 4, y: 4 (y_hi: 2, y_lo: 2; y = y_hi * 2 + y_lo), z: 8, core: 2. Of those that a mesh axis runs over, the one named last changes fastest.
Arguments:
- thermal_anomaly: float32 [8, 512, 4096], P(None, 'lat', 'lon'), may hold values from -6 to 6
- saltiness_anomaly: float32 [8, 512, 4096], P(None, 'lat', 'lon'), may hold values from -6 to 6
- eastward_flow_speed: float32 [8, 512, 4096], P(None, 'lat', 'lon'), may hold values from -3 to 3
- northward_flow_speed: float32 [8, 512, 4096], P(None, 'lat', 'lon'), may hold values from -3 to 3
- sea_indicator_field: int32 [8, 512, 4096], P(None, 'lat', 'lon'), may hold values 0 or 1
Outputs:
- temperature_out: float32 [8, 512, 4096], P(None, 'lat', 'lon')
- salinity_out: float32 [8, 512, 4096], P(None, 'lat', 'lon')
- zonal_out: float32 [8, 512, 4096], P(None, 'lat', 'lon')
- merid_out: float32 [8, 512, 4096], P(None, 'lat', 'lon')
The draws below stay inside these ranges and needn't reach their ends.
All inputs are finite; a program needn't handle non-finite values. No bound on the sum of `sea_indicator_field` on one device may be relied on, other than what follows from the above.
Results may differ from the reference program's by a relative error of at most 0.00002.
Values sent between devices are 32-bit elements; how exact they have to be, the bound alone decides.
No kernel may reach another device: no remote copies, remote signals or barrier semaphores. Data moves between devices by JAX's collectives and lax.ppermute only.
A program may use at most 64 MiB of HBM per device.

```python
import jax
import jax.numpy as jnp

VERTICAL_LAYERS = 8
NSUB = 4
NORTH_SOUTH_LINES = 512
EAST_WEST_LINES = 4096


def place_ends(values, rng, smallest, top_value):
    spot = [jax.random.randint(jax.random.fold_in(rng, axis), (), 0, length) for axis, length in enumerate(values.shape)]
    longest = values.shape.index(max(values.shape))
    beside = spot[:longest] + [(spot[longest] + 1) % values.shape[longest]] + spot[longest + 1:]
    return values.at[tuple(spot)].set(smallest).at[tuple(beside)].set(top_value)


def block_levels(stream_key, shape, cuts, least, top_value):
    def one(position, shards_of):
        heights = jax.random.uniform(jax.random.fold_in(jax.random.fold_in(stream_key, 6), position), (shards_of,), jnp.float32, least / len(cuts), top_value / len(cuts))
        return jnp.repeat(jnp.exp(heights), shape[position] // shards_of).reshape((-1,) + (1,) * (len(shape) - position - 1))

    loudness = one(*cuts[0])
    for cut in cuts[1:]:
        loudness = loudness * one(*cut)
    return loudness


def centred(stream_key, extent, deviation, bound, split=(), held_as=jnp.bfloat16):
    values = jax.random.normal(stream_key, extent, jnp.float32) * deviation
    if len(split) > 0:
        values = block_levels(stream_key, extent, split, -0.22, 0.18) * values
    return jnp.clip(values, min=-bound, max=bound).astype(held_as)


def setup_inputs(seed: int = 0) -> dict:
    keys = jax.random.split(jax.random.key(seed), 6)
    thermal_anomaly = centred(keys[0], (VERTICAL_LAYERS, NORTH_SOUTH_LINES, EAST_WEST_LINES), 1.0, 6.0, ((1, 8), (2, 32)), jnp.float32)
    saltiness_anomaly = centred(keys[1], (VERTICAL_LAYERS, NORTH_SOUTH_LINES, EAST_WEST_LINES), 1.0, 6.0, ((1, 8), (2, 32)), jnp.float32)
    eastward_flow_speed = centred(keys[2], (VERTICAL_LAYERS, NORTH_SOUTH_LINES, EAST_WEST_LINES), 0.5, 3.0, ((1, 8), (2, 32)), jnp.float32)
    northward_flow_speed = centred(keys[3], (VERTICAL_LAYERS, NORTH_SOUTH_LINES, EAST_WEST_LINES), 0.5, 3.0, ((1, 8), (2, 32)), jnp.float32)
    sea_indicator_field = place_ends((jax.random.randint(keys[4], (VERTICAL_LAYERS, NORTH_SOUTH_LINES, EAST_WEST_LINES), 0, 5) < 4).astype(jnp.int32), jax.random.fold_in(keys[4], 1), 0, 1)
    return {"thermal_anomaly": thermal_anomaly, "saltiness_anomaly": saltiness_anomaly, "eastward_flow_speed": eastward_flow_speed, "northward_flow_speed": northward_flow_speed, "sea_indicator_field": sea_indicator_field}


ADVECT = 0.25
DIFFUSE = 0.08
PRESS_COEF = 0.3
DRAG_COEF = 0.05
VISCOSITY = 0.08


def density(temper, saltiness_anomaly):
    depth = (jnp.arange(VERTICAL_LAYERS, dtype=jnp.float32)[:, None, None] + 0.5) / VERTICAL_LAYERS
    return 0.8 * saltiness_anomaly - 0.25 * temper - 0.06 * temper * temper + 0.03 * temper * saltiness_anomaly - 0.1 * depth * temper


def pressure(rho):
    return 0.2 * jnp.cumsum(rho, axis=0) - 0.1 * rho


def centre(field):
    return field[:, 1:-1, 1:-1]


def to_east(field):
    return field[:, 1:-1, 2:]


def to_west(field):
    return field[:, 1:-1, :-2]


def to_north(field):
    return field[:, 2:, 1:-1]


def to_south(field):
    return field[:, :-2, 1:-1]


def advance(extended, mask_ext, coriolis):
    temper, saltiness_anomaly, zonal, merid = extended[0], extended[1], extended[2], extended[3]
    ocean = centre(mask_ext)
    open_east = ocean * to_east(mask_ext)
    open_west = ocean * to_west(mask_ext)
    open_north = ocean * to_north(mask_ext)
    open_south = ocean * to_south(mask_ext)
    press_field = pressure(density(temper, saltiness_anomaly))
    flow_east = 0.5 * (centre(zonal) + to_east(zonal)) * open_east
    flow_west = 0.5 * (to_west(zonal) + centre(zonal)) * open_west
    flow_north = 0.5 * (centre(merid) + to_north(merid)) * open_north
    flow_south = 0.5 * (to_south(merid) + centre(merid)) * open_south

    def spread(tracer):
        middle = centre(tracer)
        return (open_east * (to_east(tracer) - middle) + open_west * (to_west(tracer) - middle)
                + open_north * (to_north(tracer) - middle) + open_south * (to_south(tracer) - middle))

    def carried(tracer):
        middle = centre(tracer)
        return (flow_east * 0.5 * (middle + to_east(tracer)) - flow_west * 0.5 * (to_west(tracer) + middle)
                + flow_north * 0.5 * (middle + to_north(tracer)) - flow_south * 0.5 * (to_south(tracer) + middle))

    new_temp = centre(temper) + ocean * (DIFFUSE * spread(temper) - ADVECT * carried(temper))
    new_salt = centre(saltiness_anomaly) + ocean * (DIFFUSE * spread(saltiness_anomaly) - ADVECT * carried(saltiness_anomaly))
    middle_p = centre(press_field)
    grad_lon = 0.5 * (open_east * (to_east(press_field) - middle_p) + open_west * (middle_p - to_west(press_field)))
    grad_lat = 0.5 * (open_north * (to_north(press_field) - middle_p) + open_south * (middle_p - to_south(press_field)))
    zonal_mid = centre(zonal)
    merid_mid = centre(merid)
    new_zonal = zonal_mid + ocean * (coriolis * merid_mid - PRESS_COEF * grad_lon - DRAG_COEF * zonal_mid + VISCOSITY * spread(zonal))
    new_merid = merid_mid + ocean * (-coriolis * zonal_mid - PRESS_COEF * grad_lat - DRAG_COEF * merid_mid + VISCOSITY * spread(merid))
    return jnp.stack([new_temp, new_salt, new_zonal, new_merid])


def extend(fields, signs):
    parallel_lines_number = fields.shape[2]
    lonpad = jnp.concatenate([fields[..., -1:], fields, fields[..., :1]], axis=3)
    folded = fields[:, :, parallel_lines_number - 1, ::-1] * signs[:, None, None]
    north_row = jnp.pad(folded[:, :, None, :], ((0, 0), (0, 0), (0, 0), (1, 1)))
    south_row = jnp.zeros_like(north_row)
    return jnp.concatenate([south_row, lonpad, north_row], axis=2)


def reference(thermal_anomaly, saltiness_anomaly, eastward_flow_speed, northward_flow_speed, sea_indicator_field):
    solver_snapshot = jnp.stack([thermal_anomaly, saltiness_anomaly, eastward_flow_speed, northward_flow_speed])
    ocean_mask = sea_indicator_field.astype(jnp.float32)
    mask_ext = extend(ocean_mask[None], jnp.ones((1,), dtype=jnp.float32))[0]
    signs = jnp.array([1.0, 1.0, -1.0, -1.0], dtype=jnp.float32)
    coriolis = (0.1 + 0.3 * (jnp.arange(NORTH_SOUTH_LINES, dtype=jnp.float32) + 0.5) / NORTH_SOUTH_LINES)[None, :, None]
    for substep in range(NSUB):
        solver_snapshot = advance(extend(solver_snapshot, signs), mask_ext, coriolis)
    return solver_snapshot[0], solver_snapshot[1], solver_snapshot[2], solver_snapshot[3]
```

```python
import functools

import jax
import jax.numpy as jnp
from jax import lax
from jax.experimental import pallas as pl
from jax.experimental.pallas import tpu as pltpu
from jax.sharding import PartitionSpec as P

NSUB = 4
LEVELS = 8
ROWS = 64
LANES = 128
CHUNKS = ROWS // 8
AXES = ("lat", "lon")

FACE = 0.08
PSCALE = 0.15 / 0.08
ASCALE = 0.0625 / 0.08
DRAG = 0.05
VMEM = 48 * 1024 * 1024


def lane_roll(x, amount):
    amount %= LANES
    return x if amount == 0 else pltpu.roll(x, amount, axis=x.ndim - 1)


def row_roll(x, amount):
    return pltpu.roll(x, amount, axis=x.ndim - 2)


def lane_index(rows=8):
    return lax.broadcasted_iota(jnp.int32, (rows, LANES), 1)


def row_index():
    return lax.broadcasted_iota(jnp.int32, (8, LANES), 0)


def density_tenth(temper, salt, depth):
    c = PSCALE * 0.1
    return salt * (c * 0.8 + (c * 0.03) * temper) - temper * (
        (c * 0.25 + c * 0.1 * depth) + (c * 0.06) * temper
    )


def along_faces(k, now, nxt, normal, press_now, press_nxt):
    t0, s0, t1, s1 = now[0], now[1], nxt[0], nxt[1]
    a = ASCALE * (now[normal] + nxt[normal])
    less = k * (1.0 - a)
    more = k * (1.0 + a)
    ft = less * t1 - more * t0
    fs = less * s1 - more * s0
    dn = nxt[normal] - now[normal]
    dp = press_nxt - press_now
    tang = 5 - normal
    ftang = k * (nxt[tang] - now[tang])
    ahead = k * (dn - dp)
    behind = k * (dn + dp)
    return ft, fs, ftang, ahead, behind


def combine(now, ocean, coriolis, east, west, north, south):
    t, s, u, v = now
    nt = t + ((east[0] - west[0]) + (north[0] - south[0]))
    ns = s + ((east[1] - west[1]) + (north[1] - south[1]))
    nu = u + (ocean * (coriolis * v - DRAG * u) + ((east[3] - west[4]) + (north[2] - south[2])))
    nv = v + (ocean * (-coriolis * u - DRAG * v) + ((east[2] - west[2]) + (north[3] - south[4])))
    return nt, ns, nu, nv


def coriolis_rows(first_row, total, shape, start):
    row = first_row + start + lax.broadcasted_iota(jnp.int32, shape, len(shape) - 2)
    row = jnp.where(row >= total, 2 * total - 1 - row, row).astype(jnp.float32)
    return 0.1 + 0.3 * (row + 0.5) / total


def pack_rows_body(count, *refs):
    low, high, (to_a, to_b) = refs[:5], refs[5:10], refs[10:]
    odd = lax.rem(lax.axis_index("lat"), 2) == 1
    upper = row_index() < 4
    for f in range(5):
        for m in range(LEVELS // 2):
            b0, b1 = low[f][2 * m], low[f][2 * m + 1]
            t0, t1 = high[f][2 * m], high[f][2 * m + 1]
            if f == 4:
                b0, b1, t0, t1 = (w.astype(jnp.float32) for w in (b0, b1, t0, t1))
            bottom = jnp.where(upper, b0, row_roll(b1, 4))
            top = jnp.where(upper, row_roll(t0, 4), t1)
            to_a[f, m] = jnp.where(odd, bottom, top)
            to_b[f, m] = jnp.where(odd, top, bottom)


def pack_rows(fields):
    lows = [pl.BlockSpec((LEVELS, 8, LANES), lambda i: (0, 0, 0)) for _ in fields]
    highs = [pl.BlockSpec((LEVELS, 8, LANES), lambda i: (0, CHUNKS - 1, 0)) for _ in fields]
    out = jax.ShapeDtypeStruct((5, LEVELS // 2, 8, LANES), jnp.float32)
    return pl.pallas_call(
        functools.partial(pack_rows_body, 0),
        grid=(1,),
        in_specs=lows + highs,
        out_specs=[pl.BlockSpec(out.shape, lambda i: (0, 0, 0, 0))] * 2,
        out_shape=[out, out],
        name="pack_rows",
    )(*fields, *fields)


def strip_of(levels):
    lane = lane_index()
    place = lane % 32
    group = lane // 32
    total = jnp.zeros((8, LANES), jnp.float32)
    for g, block in enumerate(levels):
        east = lane_roll(block, 32 * g + 4 - 120)
        west = lane_roll(block, 32 * g + 20)
        mine = group == g
        total = jnp.where(mine & (place >= 4) & (place < 12), east, total)
        total = jnp.where(mine & (place >= 20) & (place < 28), west, total)
    return total


def squeeze(tiles, start):
    place = lane_index() % 32
    total = jnp.zeros((8, LANES), jnp.float32)
    for n, tile in enumerate(tiles):
        if tile is None:
            continue
        total = jnp.where((place >= 4 * n) & (place < 4 * n + 4), lane_roll(tile, 4 * n - start), total)
    return total


def pack_columns_body(*refs):
    fields, (strips, to_e, to_w) = refs[:5], refs[5:]
    slots = {}
    for i in range(CHUNKS):
        rows = pl.ds(8 * i, 8)
        tiles = []
        for f in range(5):
            for t in range(2):
                tile = strip_of([fields[f][4 * t + g, rows].astype(jnp.float32) for g in range(4)])
                strips[f, t, rows] = tile
                tiles.append(tile)
        to_e[i] = squeeze(tiles[:8], 8)
        to_w[i] = squeeze(tiles[:8], 20)
        slots.setdefault(i // 4, []).extend(tiles[8:])
    for j in range(CHUNKS // 4):
        to_e[CHUNKS + j] = squeeze(slots[j], 8)
        to_w[CHUNKS + j] = squeeze(slots[j], 20)


def pack_columns(fields):
    part = jax.ShapeDtypeStruct((CHUNKS + CHUNKS // 4, 8, LANES), jnp.float32)
    return pl.pallas_call(
        pack_columns_body,
        out_shape=[jax.ShapeDtypeStruct((5, 2, ROWS, LANES), jnp.float32), part, part],
        compiler_params=pltpu.CompilerParams(vmem_limit_bytes=VMEM),
        cost_estimate=pl.CostEstimate(flops=20_000_000, bytes_accessed=2_000_000, transcendentals=0),
        name="pack_columns",
    )(*fields)


def mirrored(x):
    row, lane = row_index(), lane_index()
    for bit in (1, 2):
        x = jnp.where((row & bit) == 0, row_roll(x, 8 - bit), row_roll(x, bit))
    for bit in (1, 2, 4, 8, 16, 32):
        x = jnp.where((lane & bit) == 0, lane_roll(x, -bit), lane_roll(x, bit))
    return lane_roll(x, 64)


def assemble_body(from_a, from_b, part_e, part_w, halo, strips, to_e, to_w):
    lat = lax.axis_index("lat")
    odd = lax.rem(lat, 2) == 1
    at_top = lat == lax.axis_size("lat") - 1
    upper = row_index() < 4

    @pl.when(at_top)
    def _():
        for f in range(5):
            for m in range(LEVELS // 2):
                south = row_roll(from_a[f, m], 4)
                north = mirrored(from_b[f, m])
                if f in (2, 3):
                    north = -north
                halo[f, 2 * m] = jnp.where(upper, north, south)
                halo[f, 2 * m + 1] = jnp.where(upper, row_roll(north, 4), row_roll(south, 4))

    @pl.when(jnp.logical_not(at_top))
    def _():
        for f in range(5):
            for m in range(LEVELS // 2):
                a, b = from_a[f, m], from_b[f, m]
                north = jnp.where(odd, b, a)
                south = row_roll(jnp.where(odd, a, b), 4)
                halo[f, 2 * m] = jnp.where(upper, north, south)
                halo[f, 2 * m + 1] = jnp.where(upper, row_roll(north, 4), row_roll(south, 4))

    tiles = []
    for f in range(5):
        for t in range(2):
            tile = strip_of([halo[f, 4 * t + g] for g in range(4)])
            strips[f, t] = tile
            tiles.append(tile)
    for part, out, start in ((part_e, to_e, 8), (part_w, to_w, 20)):
        for i in range(CHUNKS):
            out[i] = part[i]
        out[CHUNKS] = squeeze(tiles[:8], start)
        for j in range(CHUNKS // 4):
            out[CHUNKS + 1 + j] = part[CHUNKS + j]
        out[CHUNKS + 1 + CHUNKS // 4] = squeeze(tiles[8:], start)


def assemble(from_a, from_b, part_e, part_w):
    whole = jax.ShapeDtypeStruct((CHUNKS + 2 + CHUNKS // 4, 8, LANES), jnp.float32)
    return pl.pallas_call(
        assemble_body,
        out_shape=[
            jax.ShapeDtypeStruct((5, LEVELS, 8, LANES), jnp.float32),
            jax.ShapeDtypeStruct((5, 2, 8, LANES), jnp.float32),
            whole,
            whole,
        ],
        name="assemble",
    )(from_a, from_b, part_e, part_w)


PADDED = ROWS + 16
TALL = PADDED + 8


def main_body(*refs):
    fields, halo, outs = refs[:5], refs[5], refs[6:10]
    state, press, face_e, face_n, wet, past, turn = refs[10:]
    lat = lax.axis_index("lat")
    total = ROWS * lax.axis_size("lat")
    turn[...] = coriolis_rows(lat * ROWS, total, (PADDED, LANES), -8)

    def load_in(k, _):
        for f in range(4):
            state[0, f, k, 0:8] = halo[f, k]
            state[0, f, k, 8 : 8 + ROWS] = fields[f][k]
            state[0, f, k, 8 + ROWS : PADDED] = halo[f, k]
        wet[k, 0:8] = halo[4, k]
        wet[k, 8 : 8 + ROWS] = fields[4][k].astype(jnp.float32)
        wet[k, 8 + ROWS : PADDED] = halo[4, k]
        return 0

    lax.fori_loop(0, LEVELS, load_in, 0)

    def load_faces(k, _):
        here = wet[k, 0:PADDED]
        face_e[k] = FACE * (here * lane_roll(here, -1))
        face_n[k] = FACE * (here * wet[k, 1 : PADDED + 1])
        return 0

    lax.fori_loop(0, LEVELS, load_faces, 0)

    def pressure(src, i, _):
        rows = pl.ds(pl.multiple_of(8 * i, 8), 8)
        base = jnp.zeros((8, LANES), jnp.float32)
        for k in range(LEVELS):
            h = density_tenth(state[src, 0, k, rows], state[src, 1, k, rows], (k + 0.5) / LEVELS)
            base = base + h
            press[k, rows] = base
            base = base + h
        return 0

    def northern(src, k, i, now, p0):
        after = pl.ds(8 * i + 1, 8)
        nxt = [state[src, f, k, after] for f in range(4)]
        return along_faces(face_n[k, pl.ds(8 * i, 8)], now, nxt, 3, p0, press[k, after])

    def update(src, store, i, _):
        rows = pl.ds(8 * i, 8)
        f = turn[rows]
        for k in range(LEVELS):
            now = [state[src, q, k, rows] for q in range(4)]
            p0 = press[k, rows]
            east = along_faces(
                face_e[k, rows], now, [lane_roll(q, -1) for q in now], 2, p0, lane_roll(p0, -1)
            )
            west = [
                lane_roll(east[0], 1),
                lane_roll(east[1], 1),
                lane_roll(east[2], 1),
                None,
                lane_roll(east[4], 1),
            ]
            north = northern(src, k, i, now, p0)
            for n in (0, 1, 2, 4):
                past[n, k, pl.ds(8 + 8 * i, 8)] = north[n]
            south = [None if n == 3 else past[n, k, pl.ds(7 + 8 * i, 8)] for n in range(5)]
            store(k, i, combine(now, wet[k, rows], f, east, west, north, south))
        return 0

    for step in range(NSUB):
        src = step % 2
        for i in range(CHUNKS + 2):
            pressure(src, i, 0)
        if step < NSUB - 1:

            def store(k, i, new):
                for q in range(4):
                    state[1 - src, q, k, pl.ds(8 * i, 8)] = new[q]

            for i in range(CHUNKS + 2):
                update(src, store, i, 0)
        else:

            def store(k, i, new):
                for q in range(4):
                    outs[q][k, pl.ds(8 * (i - 1), 8)] = new[q]

            for k in range(LEVELS):
                now = [state[src, q, k, 0:8] for q in range(4)]
                north = northern(src, k, 0, now, press[k, 0:8])
                for n in (0, 1, 2, 4):
                    past[n, k, 8:16] = north[n]
            for i in range(1, CHUNKS + 1):
                update(src, store, i, 0)


def main_block(fields, halo):
    out = jax.ShapeDtypeStruct((LEVELS, ROWS, LANES), jnp.float32)
    f32 = jnp.float32
    return pl.pallas_call(
        main_body,
        out_shape=[out] * 4,
        scratch_shapes=[
            pltpu.VMEM((2, 4, LEVELS, TALL, LANES), f32),
            pltpu.VMEM((LEVELS, TALL, LANES), f32),
            pltpu.VMEM((LEVELS, PADDED, LANES), f32),
            pltpu.VMEM((LEVELS, PADDED, LANES), f32),
            pltpu.VMEM((LEVELS, TALL, LANES), f32),
            pltpu.VMEM((5, LEVELS, TALL, LANES), f32),
            pltpu.VMEM((PADDED, LANES), f32),
        ],
        compiler_params=pltpu.CompilerParams(vmem_limit_bytes=VMEM),
        cost_estimate=pl.CostEstimate(flops=300_000_000, bytes_accessed=20_000_000, transcendentals=0),
        name="main_block",
    )(*fields, halo)


def strips_body(own, own_halo, from_w, from_e, *refs):
    mains, outs = refs[:4], refs[4:8]
    state, wet, turn = refs[8:]
    lat = lax.axis_index("lat")
    total = ROWS * lax.axis_size("lat")
    turn[...] = coriolis_rows(lat * ROWS, total, (PADDED, LANES), -8)
    place = lane_index() % 32
    halo_w = (place >= 16) & (place < 20)
    halo_e = (place >= 12) & (place < 16)

    def put(f, t, i, tile):
        targets = [1 + i] if i < CHUNKS else [0, CHUNKS + 1]
        for c in targets:
            if f < 4:
                state[0, f, t, 8 * c : 8 * c + 8] = tile
            else:
                wet[t, 8 * c : 8 * c + 8] = tile

    for i in range(CHUNKS + 1):
        for f in range(5):
            for t in range(2):
                tile = own[f, t, 8 * i : 8 * i + 8] if i < CHUNKS else own_halo[f, t]
                if f < 4:
                    slot, chunk = 2 * f + t, i
                else:
                    slot, chunk = 2 * (i % 4) + t, CHUNKS + 1 + i // 4
                tile = jnp.where(halo_w, lane_roll(from_w[chunk], 16 - 4 * slot), tile)
                tile = jnp.where(halo_e, lane_roll(from_e[chunk], 12 - 4 * slot), tile)
                put(f, t, i, tile)

    lane = lane_index(PADDED)
    group = lane // 32

    for step in range(NSUB):
        src = step % 2
        press = []
        whole = None
        for t in range(2):
            depth = (4 * t + group + 0.5) / LEVELS
            h = density_tenth(state[src, 0, t, 0:PADDED], state[src, 1, t, 0:PADDED], depth)
            inc = h + jnp.where(group >= 1, lane_roll(h, 32), 0.0)
            inc = inc + jnp.where(group >= 2, lane_roll(inc, 64), 0.0)
            p = 2.0 * inc - h
            if t == 0:
                whole = h + lane_roll(h, 32)
                whole = whole + lane_roll(whole, 64)
            else:
                p = p + 2.0 * whole
            press.append(p)
        for t in range(2):
            now = [state[src, f, t, 0:PADDED] for f in range(4)]
            here = wet[t, 0:PADDED]
            up = lambda q: row_roll(q, PADDED - 1)
            down = lambda q: row_roll(q, 1)
            east_face = FACE * (here * lane_roll(here, -1))
            north_face = FACE * (here * up(here))
            p0 = press[t]
            east = along_faces(east_face, now, [lane_roll(q, -1) for q in now], 2, p0, lane_roll(p0, -1))
            west = [lane_roll(q, 1) for q in east]
            north = along_faces(north_face, now, [up(q) for q in now], 3, p0, up(p0))
            south = [down(q) for q in north]
            new = combine(now, here, turn[...], east, west, north, south)
            for f in range(4):
                state[1 - src, f, t, 0:PADDED] = new[f]

    src = NSUB % 2
    lane = lane_index(ROWS)
    for f in range(4):
        for k in range(LEVELS):
            tile = state[src, f, k // 4, 8 : 8 + ROWS]
            g = 32 * (k % 4)
            block = mains[f][k]
            block = jnp.where(lane < 4, lane_roll(tile, -(g + 20)), block)
            block = jnp.where(lane >= LANES - 4, lane_roll(tile, 124 - (g + 8)), block)
            outs[f][k] = block


def strips_and_merge(own, own_halo, from_w, from_e, mains):
    out = jax.ShapeDtypeStruct((LEVELS, ROWS, LANES), jnp.float32)
    f32 = jnp.float32
    return pl.pallas_call(
        strips_body,
        out_shape=[out] * 4,
        scratch_shapes=[
            pltpu.VMEM((2, 4, 2, PADDED, LANES), f32),
            pltpu.VMEM((2, PADDED, LANES), f32),
            pltpu.VMEM((PADDED, LANES), f32),
        ],
        compiler_params=pltpu.CompilerParams(vmem_limit_bytes=VMEM),
        name="strips_and_merge",
    )(own, own_halo, from_w, from_e, *mains)


def lat_routes(lats, lons):
    first, second = [], []
    for j in range(lons):
        for i in range(lats):
            first.append((i * lons + j, (i ^ 1) * lons + j))
        for i in range(1, lats - 1):
            other = i + 1 if i % 2 else i - 1
            second.append((i * lons + j, other * lons + j))
        second.append(((lats - 1) * lons + j, (lats - 1) * lons + lons - 1 - j))
    return first, second


def on_device(*args):
    lats, lons = lax.axis_size("lat"), lax.axis_size("lon")
    route_a, route_b = lat_routes(lats, lons)
    to_a, to_b = pack_rows(args)
    from_b = lax.ppermute(to_b, AXES, route_b)
    from_a = lax.ppermute(to_a, AXES, route_a)
    own, part_e, part_w = pack_columns(args)
    halo, own_halo, to_e, to_w = assemble(from_a, from_b, part_e, part_w)
    from_w = lax.ppermute(to_e, "lon", [(i, (i + 1) % lons) for i in range(lons)])
    from_e = lax.ppermute(to_w, "lon", [((i + 1) % lons, i) for i in range(lons)])
    mains = main_block(args, halo)
    return tuple(strips_and_merge(own, own_halo, from_w, from_e, mains))


def solution(mesh):
    spec = P(None, "lat", "lon")
    return jax.shard_map(
        on_device,
        mesh=mesh,
        in_specs=(spec,) * 5,
        out_specs=(spec,) * 4,
        check_vma=False,
    )
```

```python
import functools

import jax
import jax.numpy as jnp
from jax import lax
from jax.experimental import pallas as pl
from jax.experimental.pallas import tpu as pltpu
from jax.sharding import PartitionSpec as P

NSUB = 4
LEVELS = 8
ROWS = 64
LANES = 128
CHUNKS = ROWS // 8
AXES = ("lat", "lon")

FACE = 0.08
PSCALE = 0.15 / 0.08
ASCALE = 0.0625 / 0.08
DRAG = 0.05
VMEM = 24 * 1024 * 1024
SMALL = 4 * 1024 * 1024


def lane_roll(x, amount):
    amount %= LANES
    return x if amount == 0 else pltpu.roll(x, amount, axis=x.ndim - 1)


def row_roll(x, amount):
    return pltpu.roll(x, amount, axis=x.ndim - 2)


def lane_index(rows=8):
    return lax.broadcasted_iota(jnp.int32, (rows, LANES), 1)


def row_index():
    return lax.broadcasted_iota(jnp.int32, (8, LANES), 0)


def density_tenth(temper, salt, depth):
    c = PSCALE * 0.1
    return salt * (c * 0.8 + (c * 0.03) * temper) - temper * (
        (c * 0.25 + c * 0.1 * depth) + (c * 0.06) * temper
    )


def along_faces(k, now, nxt, normal, press_now, press_nxt):
    t0, s0, t1, s1 = now[0], now[1], nxt[0], nxt[1]
    a = ASCALE * (now[normal] + nxt[normal])
    less = k * (1.0 - a)
    more = k * (1.0 + a)
    ft = less * t1 - more * t0
    fs = less * s1 - more * s0
    dn = nxt[normal] - now[normal]
    dp = press_nxt - press_now
    tang = 5 - normal
    ftang = k * (nxt[tang] - now[tang])
    ahead = k * (dn - dp)
    behind = k * (dn + dp)
    return ft, fs, ftang, ahead, behind


def combine(now, ocean, coriolis, east, west, north, south):
    t, s, u, v = now
    nt = t + ((east[0] - west[0]) + (north[0] - south[0]))
    ns = s + ((east[1] - west[1]) + (north[1] - south[1]))
    nu = u + (ocean * (coriolis * v - DRAG * u) + ((east[3] - west[4]) + (north[2] - south[2])))
    nv = v + (ocean * (-coriolis * u - DRAG * v) + ((east[2] - west[2]) + (north[3] - south[4])))
    return nt, ns, nu, nv


def coriolis_rows(first_row, total, shape, start):
    row = first_row + start + lax.broadcasted_iota(jnp.int32, shape, len(shape) - 2)
    row = jnp.where(row >= total, 2 * total - 1 - row, row).astype(jnp.float32)
    return 0.1 + 0.3 * (row + 0.5) / total


def pack_rows_body(*refs):
    fields, (to_a, to_b), (low, high, low_mask, high_mask, arrived) = refs[:5], refs[5:7], refs[7:]
    odd = lax.rem(lax.axis_index("lat"), 2) == 1
    upper = row_index() < 4
    copies = []
    for f in range(5):
        for n, (start, held, mask) in enumerate(((0, low, low_mask), (ROWS - 8, high, high_mask))):
            source = fields[f].at[:, pl.ds(start, 8), :]
            target = held.at[f] if f < 4 else mask
            copies.append(pltpu.make_async_copy(source, target, arrived.at[2 * f + n]))
    for copy in copies:
        copy.start()
    for f in range(5):
        copies[2 * f].wait()
        copies[2 * f + 1].wait()
        for m in range(LEVELS // 2):
            if f < 4:
                b0, b1, t0, t1 = low[f, 2 * m], low[f, 2 * m + 1], high[f, 2 * m], high[f, 2 * m + 1]
            else:
                b0, b1 = low_mask[2 * m].astype(jnp.float32), low_mask[2 * m + 1].astype(jnp.float32)
                t0, t1 = high_mask[2 * m].astype(jnp.float32), high_mask[2 * m + 1].astype(jnp.float32)
            bottom = jnp.where(upper, b0, row_roll(b1, 4))
            top = jnp.where(upper, row_roll(t0, 4), t1)
            to_a[f, m] = jnp.where(odd, bottom, top)
            to_b[f, m] = jnp.where(odd, top, bottom)


def pack_rows(fields):
    out = jax.ShapeDtypeStruct((5, LEVELS // 2, 8, LANES), jnp.float32)
    return pl.pallas_call(
        pack_rows_body,
        in_specs=[pl.BlockSpec(memory_space=pltpu.HBM)] * 5,
        out_specs=[pl.BlockSpec(memory_space=pltpu.VMEM)] * 2,
        out_shape=[out, out],
        scratch_shapes=[
            pltpu.VMEM((4, LEVELS, 8, LANES), jnp.float32),
            pltpu.VMEM((4, LEVELS, 8, LANES), jnp.float32),
            pltpu.VMEM((LEVELS, 8, LANES), jnp.int32),
            pltpu.VMEM((LEVELS, 8, LANES), jnp.int32),
            pltpu.SemaphoreType.DMA((10,)),
        ],
        compiler_params=pltpu.CompilerParams(vmem_limit_bytes=SMALL),
        name="pack_rows",
    )(*[pltpu.with_memory_space_constraint(field, pltpu.HBM) for field in fields])


def strip_of(levels):
    lane = lane_index()
    place = lane % 32
    group = lane // 32
    total = jnp.zeros((8, LANES), jnp.float32)
    for g, block in enumerate(levels):
        east = lane_roll(block, 32 * g + 4 - 120)
        west = lane_roll(block, 32 * g + 20)
        mine = group == g
        total = jnp.where(mine & (place >= 4) & (place < 12), east, total)
        total = jnp.where(mine & (place >= 20) & (place < 28), west, total)
    return total


def squeeze(tiles, start):
    place = lane_index() % 32
    total = jnp.zeros((8, LANES), jnp.float32)
    for n, tile in enumerate(tiles):
        if tile is None:
            continue
        total = jnp.where((place >= 4 * n) & (place < 4 * n + 4), lane_roll(tile, 4 * n - start), total)
    return total


def pack_columns(fields, strips, to_e, to_w):
    slots = {}
    for i in range(CHUNKS):
        rows = pl.ds(8 * i, 8)
        tiles = []
        for f in range(5):
            for t in range(2):
                tile = strip_of([fields[f][4 * t + g, rows].astype(jnp.float32) for g in range(4)])
                strips[f, t, rows] = tile
                tiles.append(tile)
        to_e[i] = squeeze(tiles[:8], 8)
        to_w[i] = squeeze(tiles[:8], 20)
        slots.setdefault(i // 4, []).extend(tiles[8:])
    for j in range(CHUNKS // 4):
        to_e[CHUNKS + j] = squeeze(slots[j], 8)
        to_w[CHUNKS + j] = squeeze(slots[j], 20)


def mirrored(x):
    row = row_index()
    for bit in (1, 2):
        x = jnp.where((row & bit) == 0, row_roll(x, 8 - bit), row_roll(x, bit))
    flat = x.reshape(-1, LANES)
    back = LANES - 1 - lax.broadcasted_iota(jnp.int32, flat.shape, 1)
    return jnp.take_along_axis(flat, back, axis=1).reshape(x.shape)


def assemble_body(from_a, from_b, part_e, part_w, halo, strips, to_e, to_w):
    lat = lax.axis_index("lat")
    odd = lax.rem(lat, 2) == 1
    at_top = lat == lax.axis_size("lat") - 1
    upper = row_index() < 4
    pairs = 5 * LEVELS // 2

    def write(north, south):
        even = jnp.where(upper, north, row_roll(south, 4))
        other = jnp.where(upper, row_roll(north, 4), south)
        for n in range(pairs):
            f, m = divmod(n, LEVELS // 2)
            halo[f, 2 * m] = even[n]
            halo[f, 2 * m + 1] = other[n]

    @pl.when(at_top)
    def _():
        north = mirrored(from_b[...].reshape(pairs, 8, LANES))
        flip = LEVELS // 2 * 2
        north = jnp.concatenate([north[:flip], -north[flip : 2 * flip], north[2 * flip :]], axis=0)
        write(north, from_a[...].reshape(pairs, 8, LANES))

    @pl.when(jnp.logical_not(at_top))
    def _():
        a, b = from_a[...].reshape(pairs, 8, LANES), from_b[...].reshape(pairs, 8, LANES)
        write(jnp.where(odd, b, a), jnp.where(odd, a, b))

    tiles = []
    for f in range(5):
        for t in range(2):
            tile = strip_of([halo[f, 4 * t + g] for g in range(4)])
            strips[f, t] = tile
            tiles.append(tile)
    for part, out, start in ((part_e, to_e, 8), (part_w, to_w, 20)):
        for i in range(CHUNKS):
            out[i] = part[i]
        out[CHUNKS] = squeeze(tiles[:8], start)
        for j in range(CHUNKS // 4):
            out[CHUNKS + 1 + j] = part[CHUNKS + j]
        out[CHUNKS + 1 + CHUNKS // 4] = squeeze(tiles[8:], start)


def assemble(from_a, from_b, part_e, part_w):
    whole = jax.ShapeDtypeStruct((CHUNKS + 2 + CHUNKS // 4, 8, LANES), jnp.float32)
    return pl.pallas_call(
        assemble_body,
        out_shape=[
            jax.ShapeDtypeStruct((5, LEVELS, 8, LANES), jnp.float32),
            jax.ShapeDtypeStruct((5, 2, 8, LANES), jnp.float32),
            whole,
            whole,
        ],
        compiler_params=pltpu.CompilerParams(vmem_limit_bytes=SMALL),
        name="assemble",
    )(from_a, from_b, part_e, part_w)


def step_scratch(chunks):
    rows = 8 * chunks
    f32 = jnp.float32
    return [
        pltpu.VMEM((4, LEVELS, rows + 8, LANES), f32),
        pltpu.VMEM((4, LEVELS, rows + 8, LANES), f32),
        pltpu.VMEM((LEVELS, rows + 8, LANES), f32),
        pltpu.VMEM((5, LEVELS, rows, LANES), f32),
        pltpu.VMEM((5, LEVELS, rows + 8, LANES), f32),
        pltpu.VMEM((LEVELS, rows, LANES), f32),
        pltpu.VMEM((LEVELS, rows, LANES), f32),
        pltpu.VMEM((LEVELS, rows + 8, LANES), f32),
        pltpu.VMEM((rows, LANES), f32),
    ]


def run_substeps(chunks, state_a, state_b, press, shifted, past, face_e, face_n, wet, turn):
    rows_all = 8 * chunks

    def load_faces(k, _):
        here = wet[k, 0:rows_all]
        face_e[k] = FACE * (here * lane_roll(here, -1))
        face_n[k] = FACE * (here * wet[k, 1 : rows_all + 1])
        return 0

    lax.fori_loop(0, LEVELS, load_faces, 0)

    def shift(src):
        base = jnp.zeros((rows_all, LANES), jnp.float32)
        for k in range(LEVELS):
            h = density_tenth(src[0, k, 0:rows_all], src[1, k, 0:rows_all], (k + 0.5) / LEVELS)
            base = base + h
            press[k, 0:rows_all] = base
            for q in range(4):
                shifted[q, k] = lane_roll(src[q, k, 0:rows_all], -1)
            shifted[4, k] = lane_roll(base, -1)
            base = base + h

    def update(src, dst, i, _):
        start = pl.multiple_of(8 * i, 8)
        rows, after = pl.ds(start, 8), pl.ds(start + 1, 8)
        f = turn[rows]
        for k in range(LEVELS):
            now = [src[q, k, rows] for q in range(4)]
            p0 = press[k, rows]
            ahead = [shifted[q, k, rows] for q in range(5)]
            east = along_faces(face_e[k, rows], now, ahead[:4], 2, p0, ahead[4])
            west = [None if n == 3 else lane_roll(east[n], 1) for n in range(5)]
            nxt = [src[q, k, after] for q in range(4)]
            north = along_faces(face_n[k, rows], now, nxt, 3, p0, press[k, after])
            for n in (0, 1, 2, 4):
                past[n, k, pl.ds(start + 8, 8)] = north[n]
            south = [None if n == 3 else past[n, k, pl.ds(start + 7, 8)] for n in range(5)]
            new = combine(now, wet[k, rows], f, east, west, north, south)
            for q in range(4):
                dst[q, k, rows] = new[q]
        return 0

    def two_steps(half, _):
        shift(state_a)
        lax.fori_loop(0, chunks, functools.partial(update, state_a, state_b), 0, unroll=True)
        shift(state_b)
        lax.fori_loop(0, chunks, functools.partial(update, state_b, state_a), 0, unroll=True)
        return 0

    lax.fori_loop(0, NSUB // 2, two_steps, 0)


def main_body(*refs):
    fields, outs, packs, scratch = refs[:5], refs[5:9], refs[9:12], refs[12:]
    state, wet, turn = scratch[0], scratch[-2], scratch[-1]
    pack_columns(fields, *packs)
    lat = lax.axis_index("lat")
    turn[...] = coriolis_rows(lat * ROWS, ROWS * lax.axis_size("lat"), (ROWS, LANES), 0)

    def load_in(k, _):
        for f in range(4):
            state[f, k, 0:ROWS] = fields[f][k]
        wet[k, 0:ROWS] = fields[4][k].astype(jnp.float32)
        return 0

    lax.fori_loop(0, LEVELS, load_in, 0)
    run_substeps(CHUNKS, *scratch)

    def store_out(k, _):
        for f in range(4):
            outs[f][k] = state[f, k, 0:ROWS]
        return 0

    lax.fori_loop(0, LEVELS, store_out, 0)


def main_block(fields):
    out = jax.ShapeDtypeStruct((LEVELS, ROWS, LANES), jnp.float32)
    own = jax.ShapeDtypeStruct((5, 2, ROWS, LANES), jnp.float32)
    part = jax.ShapeDtypeStruct((CHUNKS + CHUNKS // 4, 8, LANES), jnp.float32)
    return pl.pallas_call(
        main_body,
        out_shape=[out] * 4 + [own, part, part],
        scratch_shapes=step_scratch(CHUNKS),
        compiler_params=pltpu.CompilerParams(vmem_limit_bytes=VMEM),
        cost_estimate=pl.CostEstimate(flops=300_000_000, bytes_accessed=20_000_000, transcendentals=0),
        name="main_block",
    )(*fields)


def bands_body(*refs):
    low, high, halo, out, scratch = refs[:5], refs[5:10], refs[10], refs[11], refs[12:]
    state, wet, turn = scratch[0], scratch[-2], scratch[-1]
    lat = lax.axis_index("lat")
    total = ROWS * lax.axis_size("lat")
    turn[0:16] = coriolis_rows(lat * ROWS, total, (16, LANES), -8)
    turn[16:32] = coriolis_rows(lat * ROWS, total, (16, LANES), ROWS - 8)

    def load_in(k, _):
        for f in range(4):
            state[f, k, 0:8] = halo[f, k]
            state[f, k, 8:16] = low[f][k]
            state[f, k, 16:24] = high[f][k]
            state[f, k, 24:32] = halo[f, k]
        wet[k, 0:8] = halo[4, k]
        wet[k, 8:16] = low[4][k].astype(jnp.float32)
        wet[k, 16:24] = high[4][k].astype(jnp.float32)
        wet[k, 24:32] = halo[4, k]
        return 0

    lax.fori_loop(0, LEVELS, load_in, 0)
    run_substeps(4, *scratch)

    def store_out(k, _):
        for f in range(4):
            out[f, k] = state[f, k, 8:24]
        return 0

    lax.fori_loop(0, LEVELS, store_out, 0)


def edge_specs(fields):
    low = [pl.BlockSpec((LEVELS, 8, LANES), lambda i: (0, 0, 0)) for _ in fields]
    high = [pl.BlockSpec((LEVELS, 8, LANES), lambda i: (0, CHUNKS - 1, 0)) for _ in fields]
    return low + high


def bands(fields, halo):
    out = jax.ShapeDtypeStruct((4, LEVELS, 16, LANES), jnp.float32)
    return pl.pallas_call(
        bands_body,
        grid=(1,),
        in_specs=edge_specs(fields) + [pl.BlockSpec(halo.shape, lambda i: (0, 0, 0, 0))],
        out_specs=pl.BlockSpec(out.shape, lambda i: (0, 0, 0, 0)),
        out_shape=out,
        scratch_shapes=step_scratch(4),
        compiler_params=pltpu.CompilerParams(vmem_limit_bytes=VMEM),
        cost_estimate=pl.CostEstimate(flops=100_000_000, bytes_accessed=8_000_000, transcendentals=0),
        name="bands",
    )(*fields, *fields, halo)


PADDED = ROWS + 16


def strips_body(own, own_halo, from_w, from_e, band, *refs):
    mains, outs = refs[:4], refs[4:8]
    state, wet, turn = refs[8:]
    lat = lax.axis_index("lat")
    total = ROWS * lax.axis_size("lat")
    turn[...] = coriolis_rows(lat * ROWS, total, (PADDED, LANES), -8)
    place = lane_index() % 32
    halo_w = (place >= 16) & (place < 20)
    halo_e = (place >= 12) & (place < 16)

    def put(f, t, i, tile):
        targets = [1 + i] if i < CHUNKS else [0, CHUNKS + 1]
        for c in targets:
            if f < 4:
                state[0, f, t, 8 * c : 8 * c + 8] = tile
            else:
                wet[t, 8 * c : 8 * c + 8] = tile

    for i in range(CHUNKS + 1):
        for f in range(5):
            for t in range(2):
                tile = own[f, t, 8 * i : 8 * i + 8] if i < CHUNKS else own_halo[f, t]
                if f < 4:
                    slot, chunk = 2 * f + t, i
                else:
                    slot, chunk = 2 * (i % 4) + t, CHUNKS + 1 + i // 4
                tile = jnp.where(halo_w, lane_roll(from_w[chunk], 16 - 4 * slot), tile)
                tile = jnp.where(halo_e, lane_roll(from_e[chunk], 12 - 4 * slot), tile)
                put(f, t, i, tile)

    lane = lane_index(PADDED)
    group = lane // 32

    for step in range(NSUB):
        src = step % 2
        press = []
        whole = None
        for t in range(2):
            depth = (4 * t + group + 0.5) / LEVELS
            h = density_tenth(state[src, 0, t, 0:PADDED], state[src, 1, t, 0:PADDED], depth)
            inc = h + jnp.where(group >= 1, lane_roll(h, 32), 0.0)
            inc = inc + jnp.where(group >= 2, lane_roll(inc, 64), 0.0)
            p = 2.0 * inc - h
            if t == 0:
                whole = h + lane_roll(h, 32)
                whole = whole + lane_roll(whole, 64)
            else:
                p = p + 2.0 * whole
            press.append(p)
        for t in range(2):
            now = [state[src, f, t, 0:PADDED] for f in range(4)]
            here = wet[t, 0:PADDED]
            up = lambda q: row_roll(q, PADDED - 1)
            down = lambda q: row_roll(q, 1)
            east_face = FACE * (here * lane_roll(here, -1))
            north_face = FACE * (here * up(here))
            p0 = press[t]
            east = along_faces(east_face, now, [lane_roll(q, -1) for q in now], 2, p0, lane_roll(p0, -1))
            west = [lane_roll(q, 1) for q in east]
            north = along_faces(north_face, now, [up(q) for q in now], 3, p0, up(p0))
            south = [down(q) for q in north]
            new = combine(now, here, turn[...], east, west, north, south)
            for f in range(4):
                state[1 - src, f, t, 0:PADDED] = new[f]

    src = NSUB % 2
    lane = lane_index(ROWS)
    upper = row_index() < 4
    for f in range(4):
        for k in range(LEVELS):
            tile = state[src, f, k // 4, 8 : 8 + ROWS]
            g = 32 * (k % 4)
            block = jnp.concatenate(
                [
                    jnp.where(upper, band[f, k, 0:8], mains[f][k, 0:8]),
                    mains[f][k, 8 : ROWS - 8],
                    jnp.where(upper, mains[f][k, ROWS - 8 : ROWS], band[f, k, 8:16]),
                ],
                axis=0,
            )
            block = jnp.where(lane < 4, lane_roll(tile, -(g + 20)), block)
            block = jnp.where(lane >= LANES - 4, lane_roll(tile, 124 - (g + 8)), block)
            outs[f][k] = block


def strips_and_merge(own, own_halo, from_w, from_e, band, mains):
    out = jax.ShapeDtypeStruct((LEVELS, ROWS, LANES), jnp.float32)
    f32 = jnp.float32
    return pl.pallas_call(
        strips_body,
        out_shape=[out] * 4,
        scratch_shapes=[
            pltpu.VMEM((2, 4, 2, PADDED, LANES), f32),
            pltpu.VMEM((2, PADDED, LANES), f32),
            pltpu.VMEM((PADDED, LANES), f32),
        ],
        compiler_params=pltpu.CompilerParams(vmem_limit_bytes=VMEM),
        name="strips_and_merge",
    )(own, own_halo, from_w, from_e, band, *mains)


def lat_routes(lats, lons):
    first, second = [], []
    for j in range(lons):
        for i in range(lats):
            first.append((i * lons + j, (i ^ 1) * lons + j))
        for i in range(1, lats - 1):
            other = i + 1 if i % 2 else i - 1
            second.append((i * lons + j, other * lons + j))
        second.append(((lats - 1) * lons + j, (lats - 1) * lons + lons - 1 - j))
    return first, second


def on_device(*args):
    lats, lons = lax.axis_size("lat"), lax.axis_size("lon")
    route_a, route_b = lat_routes(lats, lons)
    to_a, to_b = pack_rows(args)
    from_b = lax.ppermute(to_b, AXES, route_b)
    from_a = lax.ppermute(to_a, AXES, route_a)
    *mains, own, part_e, part_w = main_block(args)
    halo, own_halo, to_e, to_w = assemble(from_a, from_b, part_e, part_w)
    from_w = lax.ppermute(to_e, "lon", [(i, (i + 1) % lons) for i in range(lons)])
    from_e = lax.ppermute(to_w, "lon", [((i + 1) % lons, i) for i in range(lons)])
    band = bands(args, halo)
    return tuple(strips_and_merge(own, own_halo, from_w, from_e, band, mains))


def solution(mesh):
    spec = P(None, "lat", "lon")
    return jax.shard_map(
        on_device,
        mesh=mesh,
        in_specs=(spec,) * 5,
        out_specs=(spec,) * 4,
        check_vma=False,
    )
```

```python
import functools

import jax
import jax.numpy as jnp
from jax import lax
from jax.experimental import pallas as pl
from jax.experimental.pallas import tpu as pltpu
from jax.sharding import PartitionSpec as P

NSUB = 4
LEVELS = 8
ROWS = 64
LANES = 128
CHUNKS = ROWS // 8
AXES = ("lat", "lon")

FACE = 0.08
ASCALE = 0.0625 / 0.08
PSCALE = ASCALE * 0.15 / 0.08
DRAG = 0.05
VMEM = 24 * 1024 * 1024
SMALL = 4 * 1024 * 1024


def lane_roll(x, amount):
    amount %= LANES
    return x if amount == 0 else pltpu.roll(x, amount, axis=x.ndim - 1)


def row_roll(x, amount):
    return pltpu.roll(x, amount, axis=x.ndim - 2)


def lane_index(rows=8):
    return lax.broadcasted_iota(jnp.int32, (rows, LANES), 1)


def row_index():
    return lax.broadcasted_iota(jnp.int32, (8, LANES), 0)


def density_tenth(temper, salt, depth):
    c = PSCALE * 0.1
    return salt * (c * 0.8 + (c * 0.03) * temper) - temper * (
        (c * 0.25 + c * 0.1 * depth) + (c * 0.06) * temper
    )


def along_faces(k, now, nxt, normal, press_now, press_nxt):
    t0, s0, t1, s1 = now[0], now[1], nxt[0], nxt[1]
    a = now[normal] + nxt[normal]
    less = k * (1.0 - a)
    more = k * (1.0 + a)
    ft = less * t1 - more * t0
    fs = less * s1 - more * s0
    dn = nxt[normal] - now[normal]
    dp = press_nxt - press_now
    tang = 5 - normal
    ftang = k * (nxt[tang] - now[tang])
    ahead = k * (dn - dp)
    behind = k * (dn + dp)
    return ft, fs, ftang, ahead, behind


def combine(now, keep, turn, east, west, north, south):
    t, s, u, v = now
    nt = t + ((east[0] - west[0]) + (north[0] - south[0]))
    ns = s + ((east[1] - west[1]) + (north[1] - south[1]))
    nu = (keep * u + turn * v) + ((east[3] - west[4]) + (north[2] - south[2]))
    nv = (keep * v - turn * u) + ((east[2] - west[2]) + (north[3] - south[4]))
    return nt, ns, nu, nv


def coriolis(row):
    total = ROWS * lax.axis_size("lat")
    row = row + lax.axis_index("lat") * ROWS
    row = jnp.where(row >= total, 2 * total - 1 - row, row).astype(jnp.float32)
    return 0.1 + 0.3 * (row + 0.5) / total


def pack_rows_body(*refs):
    fields, (to_b, to_a), (low, high, low_mask, high_mask, arrived) = refs[:5], refs[5:7], refs[7:]
    odd = lax.rem(lax.axis_index("lat"), 2) == 1
    upper = row_index() < 4
    copies = []
    for f in range(5):
        for n, (start, held, mask) in enumerate(((0, low, low_mask), (ROWS - 8, high, high_mask))):
            source = fields[f].at[:, pl.ds(start, 8), :]
            target = held.at[f] if f < 4 else mask
            copies.append(pltpu.make_async_copy(source, target, arrived.at[2 * f + n]))
    for copy in copies:
        copy.start()
    for f in range(5):
        copies[2 * f].wait()
        copies[2 * f + 1].wait()
        for m in range(LEVELS // 2):
            if f < 4:
                b0, b1, t0, t1 = low[f, 2 * m], low[f, 2 * m + 1], high[f, 2 * m], high[f, 2 * m + 1]
            else:
                b0, b1 = low_mask[2 * m].astype(jnp.float32), low_mask[2 * m + 1].astype(jnp.float32)
                t0, t1 = high_mask[2 * m].astype(jnp.float32), high_mask[2 * m + 1].astype(jnp.float32)
            bottom = jnp.where(upper, b0, row_roll(b1, 4))
            top = jnp.where(upper, row_roll(t0, 4), t1)
            to_a[f, m] = jnp.where(odd, bottom, top)
            to_b[f, m] = jnp.where(odd, top, bottom)


def pack_rows(fields):
    out = jax.ShapeDtypeStruct((5, LEVELS // 2, 8, LANES), jnp.float32)
    return pl.pallas_call(
        pack_rows_body,
        in_specs=[pl.BlockSpec(memory_space=pltpu.HBM)] * 5,
        out_specs=[pl.BlockSpec(memory_space=pltpu.VMEM)] * 2,
        out_shape=[out, out],
        scratch_shapes=[
            pltpu.VMEM((4, LEVELS, 8, LANES), jnp.float32),
            pltpu.VMEM((4, LEVELS, 8, LANES), jnp.float32),
            pltpu.VMEM((LEVELS, 8, LANES), jnp.int32),
            pltpu.VMEM((LEVELS, 8, LANES), jnp.int32),
            pltpu.SemaphoreType.DMA((10,)),
        ],
        compiler_params=pltpu.CompilerParams(vmem_limit_bytes=SMALL),
        name="pack_rows",
    )(*[pltpu.with_memory_space_constraint(field, pltpu.HBM) for field in fields])


def edge_tile(levels):
    lane = lane_index()
    total = lane_roll(levels[0], 8)
    for k in range(1, LEVELS):
        total = jnp.where(lane >= 16 * k, lane_roll(levels[k], 16 * k + 8), total)
    return total


def squeeze(tiles, start):
    place = lane_index() % 16
    total = lane_roll(tiles[0], -start)
    for n in range(1, len(tiles)):
        total = jnp.where(place >= 4 * n, lane_roll(tiles[n], 4 * n - start), total)
    return total


def send_to(odd, tiles):
    east, west = squeeze(tiles, 4), squeeze(tiles, 8)
    return jnp.where(odd, west, east), jnp.where(odd, east, west)


def odd_lon():
    return lax.rem(lax.axis_index("lon"), 2) == 1


def pack_columns(fields, edges, part_b, part_a):
    odd = odd_lon()
    tiles = []
    for i in range(CHUNKS):
        rows = pl.ds(8 * i, 8)
        tiles.append([edge_tile([fields[f][k, rows].astype(jnp.float32) for k in range(LEVELS)]) for f in range(5)])
    parts = [send_to(odd, row[:4]) for row in tiles]
    for j in range(CHUNKS // 4):
        parts.append(send_to(odd, [row[4] for row in tiles[4 * j : 4 * j + 4]]))
    for i, row in enumerate(tiles):
        for f in range(5):
            edges[f, 8 * i : 8 * i + 8] = row[f]
    for n, (to_a, to_b) in enumerate(parts):
        part_a[n] = to_a
        part_b[n] = to_b


def mirrored(x):
    row = row_index()
    for bit in (1, 2):
        x = jnp.where((row & bit) == 0, row_roll(x, 8 - bit), row_roll(x, bit))
    flat = x.reshape(-1, LANES)
    back = LANES - 1 - lax.broadcasted_iota(jnp.int32, flat.shape, 1)
    return jnp.take_along_axis(flat, back, axis=1).reshape(x.shape)


def assemble_body(from_b, from_a, part_b, part_a, halo, edges, to_b, to_a):
    lat = lax.axis_index("lat")
    odd = lax.rem(lat, 2) == 1
    at_top = lat == lax.axis_size("lat") - 1
    upper = row_index() < 4
    pairs = 5 * LEVELS // 2

    def write(north, south):
        even = jnp.where(upper, north, row_roll(south, 4))
        other = jnp.where(upper, row_roll(north, 4), south)
        for n in range(pairs):
            f, m = divmod(n, LEVELS // 2)
            halo[f, 2 * m] = even[n]
            halo[f, 2 * m + 1] = other[n]

    @pl.when(at_top)
    def _():
        north = mirrored(from_b[...].reshape(pairs, 8, LANES))
        flip = LEVELS // 2 * 2
        north = jnp.concatenate([north[:flip], -north[flip : 2 * flip], north[2 * flip :]], axis=0)
        write(north, from_a[...].reshape(pairs, 8, LANES))

    @pl.when(jnp.logical_not(at_top))
    def _():
        a, b = from_a[...].reshape(pairs, 8, LANES), from_b[...].reshape(pairs, 8, LANES)
        write(jnp.where(odd, b, a), jnp.where(odd, a, b))

    tiles = []
    for f in range(5):
        tile = edge_tile([halo[f, k] for k in range(LEVELS)])
        edges[f] = tile
        tiles.append(tile)
    for part, out in ((part_a, to_a), (part_b, to_b)):
        for i in range(CHUNKS):
            out[i] = part[i]
        for j in range(CHUNKS // 4):
            out[CHUNKS + 1 + j] = part[CHUNKS + j]
    last = CHUNKS + 1 + CHUNKS // 4
    to_a[CHUNKS], to_b[CHUNKS] = send_to(odd_lon(), tiles[:4])
    to_a[last], to_b[last] = send_to(odd_lon(), tiles[4:])


def assemble(from_b, from_a, part_b, part_a):
    whole = jax.ShapeDtypeStruct((CHUNKS + 2 + CHUNKS // 4, 8, LANES), jnp.float32)
    return pl.pallas_call(
        assemble_body,
        out_shape=[
            jax.ShapeDtypeStruct((5, LEVELS, 8, LANES), jnp.float32),
            jax.ShapeDtypeStruct((5, 8, LANES), jnp.float32),
            whole,
            whole,
        ],
        compiler_params=pltpu.CompilerParams(vmem_limit_bytes=SMALL),
        name="assemble",
    )(from_b, from_a, part_b, part_a)


def step_scratch(levels, chunks):
    rows = 8 * chunks
    f32 = jnp.float32
    return [
        pltpu.VMEM((4, levels, rows + 8, LANES), f32),
        pltpu.VMEM((4, levels, rows + 8, LANES), f32),
        pltpu.VMEM((levels, rows + 8, LANES), f32),
        pltpu.VMEM((5, levels, rows, LANES), f32),
        pltpu.VMEM((5, levels, rows + 8, LANES), f32),
        pltpu.VMEM((levels, rows, LANES), f32),
        pltpu.VMEM((levels, rows, LANES), f32),
        pltpu.VMEM((levels, rows, LANES), f32),
        pltpu.VMEM((levels, rows, LANES), f32),
        pltpu.VMEM((levels, rows + 8, LANES), f32),
    ]


def pressure_by_level(rows, src):
    base = jnp.zeros((rows, LANES), jnp.float32)
    for k in range(LEVELS):
        h = density_tenth(src[0, k, 0:rows], src[1, k, 0:rows], (k + 0.5) / LEVELS)
        base = base + h
        yield base
        base = base + h


def run_substeps(
    levels, chunks, pressure, turn_rows, state_a, state_b, press, shifted, past, face_e, face_n, keep, turn, wet
):
    rows_all = 8 * chunks

    def load_faces(k, _):
        here = wet[k, 0:rows_all]
        face_e[k] = FACE * (here * lane_roll(here, -1))
        face_n[k] = FACE * (here * wet[k, 1 : rows_all + 1])
        keep[k] = 1.0 - DRAG * here
        turn[k] = here * turn_rows
        return 0

    lax.fori_loop(0, levels, load_faces, 0, unroll=True)

    def shift(src):
        for k, base in enumerate(pressure(rows_all, src)):
            press[k, 0:rows_all] = base
            for q in range(4):
                shifted[q, k] = lane_roll(src[q, k, 0:rows_all], -1)
            shifted[4, k] = lane_roll(base, -1)

    def update(src, dst, i, _):
        start = pl.multiple_of(8 * i, 8)
        rows, after = pl.ds(start, 8), pl.ds(start + 1, 8)
        for k in range(levels):
            now = [src[q, k, rows] for q in range(4)]
            p0 = press[k, rows]
            ahead = [shifted[q, k, rows] for q in range(5)]
            east = along_faces(face_e[k, rows], now, ahead[:4], 2, p0, ahead[4])
            west = [None if n == 3 else lane_roll(east[n], 1) for n in range(5)]
            nxt = [src[q, k, after] for q in range(4)]
            north = along_faces(face_n[k, rows], now, nxt, 3, p0, press[k, after])
            for n in (0, 1, 2, 4):
                past[n, k, pl.ds(start + 8, 8)] = north[n]
            south = [None if n == 3 else past[n, k, pl.ds(start + 7, 8)] for n in range(5)]
            new = combine(now, keep[k, rows], turn[k, rows], east, west, north, south)
            for q in range(4):
                dst[q, k, rows] = new[q]
        return 0

    def two_steps(half, _):
        shift(state_a)
        lax.fori_loop(0, chunks, functools.partial(update, state_a, state_b), 0, unroll=True)
        shift(state_b)
        lax.fori_loop(0, chunks, functools.partial(update, state_b, state_a), 0, unroll=True)
        return 0

    lax.fori_loop(0, NSUB // 2, two_steps, 0)


def held(f, x):
    return x * ASCALE if f in (2, 3) else x


def given(f, x):
    return x * (1.0 / ASCALE) if f in (2, 3) else x


def main_body(*refs):
    fields, outs, packs, scratch = refs[:5], refs[5:9], refs[9:12], refs[12:]
    state, wet = scratch[0], scratch[-1]
    pack_columns(fields, *packs)

    def load_in(k, _):
        for f in range(4):
            state[f, k, 0:ROWS] = held(f, fields[f][k])
        wet[k, 0:ROWS] = fields[4][k].astype(jnp.float32)
        return 0

    lax.fori_loop(0, LEVELS, load_in, 0, unroll=True)
    turn_rows = coriolis(lax.broadcasted_iota(jnp.int32, (ROWS, LANES), 0))
    run_substeps(LEVELS, CHUNKS, pressure_by_level, turn_rows, *scratch)

    def store_out(k, _):
        for f in range(4):
            outs[f][k] = given(f, state[f, k, 0:ROWS])
        return 0

    lax.fori_loop(0, LEVELS, store_out, 0, unroll=True)


def main_block(fields):
    out = jax.ShapeDtypeStruct((LEVELS, ROWS, LANES), jnp.float32)
    edges = jax.ShapeDtypeStruct((5, ROWS, LANES), jnp.float32)
    part = jax.ShapeDtypeStruct((CHUNKS + CHUNKS // 4, 8, LANES), jnp.float32)
    return pl.pallas_call(
        main_body,
        out_shape=[out] * 4 + [edges, part, part],
        scratch_shapes=step_scratch(LEVELS, CHUNKS),
        compiler_params=pltpu.CompilerParams(vmem_limit_bytes=VMEM),
        cost_estimate=pl.CostEstimate(flops=300_000_000, bytes_accessed=20_000_000, transcendentals=0),
        name="main_block",
    )(*fields)


def bands_body(*refs):
    low, high, halo, out, scratch = refs[:5], refs[5:10], refs[10], refs[11], refs[12:]
    state, wet = scratch[0], scratch[-1]

    def load_in(k, _):
        for f in range(4):
            state[f, k, 0:8] = held(f, high[f][k])
            state[f, k, 8:16] = held(f, halo[f, k])
            state[f, k, 16:24] = held(f, low[f][k])
        wet[k, 0:8] = high[4][k].astype(jnp.float32)
        wet[k, 8:16] = halo[4, k]
        wet[k, 16:24] = low[4][k].astype(jnp.float32)
        return 0

    lax.fori_loop(0, LEVELS, load_in, 0, unroll=True)
    place = lax.broadcasted_iota(jnp.int32, (24, LANES), 0)
    turn_rows = coriolis(jnp.where(place < 12, place + (ROWS - 8), place - 16))
    run_substeps(LEVELS, 3, pressure_by_level, turn_rows, *scratch)

    def store_out(k, _):
        for f in range(4):
            out[f, k, 0:8] = given(f, state[f, k, 16:24])
            out[f, k, 8:16] = given(f, state[f, k, 0:8])
        return 0

    lax.fori_loop(0, LEVELS, store_out, 0, unroll=True)


def bands(fields, halo):
    low = [pl.BlockSpec((LEVELS, 8, LANES), lambda i: (0, 0, 0)) for _ in fields]
    high = [pl.BlockSpec((LEVELS, 8, LANES), lambda i: (0, CHUNKS - 1, 0)) for _ in fields]
    out = jax.ShapeDtypeStruct((4, LEVELS, 16, LANES), jnp.float32)
    return pl.pallas_call(
        bands_body,
        grid=(1,),
        in_specs=low + high + [pl.BlockSpec(halo.shape, lambda i: (0, 0, 0, 0))],
        out_specs=pl.BlockSpec(out.shape, lambda i: (0, 0, 0, 0)),
        out_shape=out,
        scratch_shapes=step_scratch(LEVELS, 3),
        compiler_params=pltpu.CompilerParams(vmem_limit_bytes=VMEM),
        cost_estimate=pl.CostEstimate(flops=100_000_000, bytes_accessed=8_000_000, transcendentals=0),
        name="bands",
    )(*fields, *fields, halo)


TALL = CHUNKS + 2


def pressure_by_lanes(rows, src):
    group = lax.broadcasted_iota(jnp.int32, (rows, LANES), 1) // 16
    depth = (group.astype(jnp.float32) + 0.5) / LEVELS
    for t in range(2):
        h = density_tenth(src[0, t, 0:rows], src[1, t, 0:rows], depth)
        below = [jnp.where(group >= n, lane_roll(h, 16 * n), 0.0) for n in range(1, LEVELS)]
        while len(below) > 1:
            below = [sum(below[n : n + 2]) for n in range(0, len(below), 2)]
        yield 2.0 * below[0] + h


def strips_body(edges, edge_halo, from_b, from_a, band, *refs):
    mains, outs, scratch = refs[:4], refs[4:8], refs[8:18]
    merged, sent = refs[18:]
    state, wet = scratch[0], scratch[-1]
    odd = odd_lon()
    lane = lane_index()
    place = lane % 16
    east_halo = (place >= 8) & (place < 12)
    west_halo = (place >= 4) & (place < 8)
    for i in range(CHUNKS + 1):
        for f in range(5):
            slot, chunk = (f, i) if f < 4 else (i % 4, CHUNKS + 1 + i // 4)
            own = edges[f, 8 * i : 8 * i + 8] if i < CHUNKS else edge_halo[f]
            a, b = from_a[chunk], from_b[chunk]
            east = jnp.where(east_halo, lane_roll(jnp.where(odd, b, a), 8 - 4 * slot), own)
            west = jnp.where(west_halo, lane_roll(jnp.where(odd, a, b), 4 - 4 * slot), own)
            for c in [1 + i] if i < CHUNKS else [0, CHUNKS + 1]:
                for t, tile in enumerate((east, west)):
                    if f < 4:
                        state[f, t, 8 * c : 8 * c + 8] = held(f, tile)
                    else:
                        wet[t, 8 * c : 8 * c + 8] = tile

    turn_rows = coriolis(lax.broadcasted_iota(jnp.int32, (8 * TALL, LANES), 0) - 8)
    run_substeps(2, TALL, pressure_by_lanes, turn_rows, *scratch)

    upper = row_index() < 4
    outer = (lane < 4) | (lane >= LANES - 4)
    copies = []
    for f in range(4):
        for i in range(CHUNKS):
            rows = pl.ds(8 * i, 8)
            c = 8 * (i + 1)
            edge = given(f, jnp.where(place < 8, state[f, 0, c : c + 8], state[f, 1, c : c + 8]))
            for k in range(LEVELS):
                block = mains[f][k, rows]
                if i == 0:
                    block = jnp.where(upper, band[f, k, 0:8], block)
                if i == CHUNKS - 1:
                    block = jnp.where(upper, block, band[f, k, 8:16])
                merged[f, k, rows] = jnp.where(outer, lane_roll(edge, -(16 * k + 8)), block)
        for n in range(2):
            half = pl.ds(n * LEVELS // 2, LEVELS // 2)
            copies.append(pltpu.make_async_copy(merged.at[f, half], outs[f].at[half], sent.at[2 * f + n]))
            copies[-1].start()
    for copy in copies:
        copy.wait()


def strips_and_merge(edges, edge_halo, from_b, from_a, band, mains):
    out = jax.ShapeDtypeStruct((LEVELS, ROWS, LANES), jnp.float32)
    return pl.pallas_call(
        strips_body,
        out_specs=[pl.BlockSpec(memory_space=pl.ANY)] * 4,
        out_shape=[out] * 4,
        scratch_shapes=step_scratch(2, TALL)
        + [pltpu.VMEM((4, LEVELS, ROWS, LANES), jnp.float32), pltpu.SemaphoreType.DMA((8,))],
        compiler_params=pltpu.CompilerParams(vmem_limit_bytes=VMEM),
        name="strips_and_merge",
    )(edges, edge_halo, from_b, from_a, band, *mains)


def lat_routes(lats, lons):
    first, second = [], []
    for j in range(lons):
        for i in range(lats):
            first.append((i * lons + j, (i ^ 1) * lons + j))
        for i in range(1, lats - 1):
            other = i + 1 if i % 2 else i - 1
            second.append((i * lons + j, other * lons + j))
        second.append(((lats - 1) * lons + j, (lats - 1) * lons + lons - 1 - j))
    return first, second


def lon_routes(lons):
    first = [(j, j ^ 1) for j in range(lons)]
    second = [(j, (j + 1 if j % 2 else j - 1) % lons) for j in range(lons)]
    return first, second


def on_device(*args):
    route_a, route_b = lat_routes(lax.axis_size("lat"), lax.axis_size("lon"))
    to_b, to_a = pack_rows(args)
    from_b = lax.ppermute(to_b, AXES, route_b)
    from_a = lax.ppermute(to_a, AXES, route_a)
    *mains, edges, part_b, part_a = main_block(args)
    halo, edge_halo, to_b, to_a = assemble(from_b, from_a, part_b, part_a)
    route_a, route_b = lon_routes(lax.axis_size("lon"))
    from_b = lax.ppermute(to_b, "lon", route_b)
    from_a = lax.ppermute(to_a, "lon", route_a)
    band = bands(args, halo)
    return tuple(strips_and_merge(edges, edge_halo, from_b, from_a, band, mains))


def solution(mesh):
    spec = P(None, "lat", "lon")
    return jax.shard_map(
        on_device,
        mesh=mesh,
        in_specs=(spec,) * 5,
        out_specs=(spec,) * 4,
        check_vma=False,
    )
```

```python
import functools

import jax
import jax.numpy as jnp
from jax import lax
from jax.experimental import pallas as pl
from jax.experimental.pallas import tpu as pltpu
from jax.sharding import PartitionSpec as P

NSUB = 4
LEVELS = 8
ROWS = 64
LANES = 128
CHUNKS = ROWS // 8
AXES = ("lat", "lon")

FACE = 0.08
ASCALE = 0.0625 / 0.08
PSCALE = ASCALE * 0.15 / 0.08
DRAG = 0.05
VMEM = 24 * 1024 * 1024
SMALL = 4 * 1024 * 1024


def lane_roll(x, amount):
    amount %= LANES
    return x if amount == 0 else pltpu.roll(x, amount, axis=x.ndim - 1)


def row_roll(x, amount):
    return pltpu.roll(x, amount, axis=x.ndim - 2)


def lane_index(rows=8):
    return lax.broadcasted_iota(jnp.int32, (rows, LANES), 1)


def row_index():
    return lax.broadcasted_iota(jnp.int32, (8, LANES), 0)


def density_tenth(temper, salt, depth):
    c = PSCALE * 0.1
    return salt * (c * 0.8 + (c * 0.03) * temper) - temper * (
        (c * 0.25 + c * 0.1 * depth) + (c * 0.06) * temper
    )


def along_faces(k, now, nxt, normal, press_now, press_nxt):
    t0, s0, t1, s1 = now[0], now[1], nxt[0], nxt[1]
    a = now[normal] + nxt[normal]
    less = k * (1.0 - a)
    more = k * (1.0 + a)
    ft = less * t1 - more * t0
    fs = less * s1 - more * s0
    dn = nxt[normal] - now[normal]
    dp = press_nxt - press_now
    tang = 5 - normal
    ftang = k * (nxt[tang] - now[tang])
    ahead = k * (dn - dp)
    behind = k * (dn + dp)
    return ft, fs, ftang, ahead, behind


def combine(now, keep, turn, east, west, north, south):
    t, s, u, v = now
    nt = t + ((east[0] - west[0]) + (north[0] - south[0]))
    ns = s + ((east[1] - west[1]) + (north[1] - south[1]))
    nu = (keep * u + turn * v) + ((east[3] - west[4]) + (north[2] - south[2]))
    nv = (keep * v - turn * u) + ((east[2] - west[2]) + (north[3] - south[4]))
    return nt, ns, nu, nv


def coriolis(row):
    total = ROWS * lax.axis_size("lat")
    row = row + lax.axis_index("lat") * ROWS
    row = jnp.where(row >= total, 2 * total - 1 - row, row).astype(jnp.float32)
    return 0.1 + 0.3 * (row + 0.5) / total


def pack_pairs(take, top, out):
    upper = row_index() < 4
    for f in range(5):
        for m in range(LEVELS // 2):
            first, second = take(f, 2 * m), take(f, 2 * m + 1)
            lows = jnp.where(upper, first, row_roll(second, 4))
            highs = jnp.where(upper, row_roll(first, 4), second)
            out[f, m] = jnp.where(top, highs, lows)


def odd_lat():
    return lax.rem(lax.axis_index("lat"), 2) == 1


def pack_rows_body(*refs):
    fields, out, (held_rows, held_mask, arrived) = refs[:5], refs[5], refs[6:]
    start = pl.multiple_of(jnp.where(odd_lat(), ROWS - 8, 0), 8)
    copies = []
    for f in range(5):
        target = held_rows.at[f] if f < 4 else held_mask
        copies.append(pltpu.make_async_copy(fields[f].at[:, pl.ds(start, 8), :], target, arrived.at[f]))
    for copy in copies:
        copy.start()
    for copy in copies:
        copy.wait()
    pack_pairs(
        lambda f, k: held_rows[f, k] if f < 4 else held_mask[k].astype(jnp.float32), odd_lat(), out
    )


def pack_rows(fields):
    return pl.pallas_call(
        pack_rows_body,
        in_specs=[pl.BlockSpec(memory_space=pltpu.HBM)] * 5,
        out_specs=pl.BlockSpec(memory_space=pltpu.VMEM),
        out_shape=jax.ShapeDtypeStruct((5, LEVELS // 2, 8, LANES), jnp.float32),
        scratch_shapes=[
            pltpu.VMEM((4, LEVELS, 8, LANES), jnp.float32),
            pltpu.VMEM((LEVELS, 8, LANES), jnp.int32),
            pltpu.SemaphoreType.DMA((5,)),
        ],
        compiler_params=pltpu.CompilerParams(vmem_limit_bytes=SMALL),
        name="pack_rows",
    )(*[pltpu.with_memory_space_constraint(field, pltpu.HBM) for field in fields])


def edge_tile(levels):
    lane = lane_index()
    total = lane_roll(levels[0], 8)
    for k in range(1, LEVELS):
        total = jnp.where(lane >= 16 * k, lane_roll(levels[k], 16 * k + 8), total)
    return total


def send_to(odd, tiles):
    place = lane_index() % 16
    rolled = [lane_roll(tile, 4 * n - 8) for n, tile in enumerate(tiles)]
    west = east = rolled[0]
    for n in range(1, len(tiles)):
        west = jnp.where(place >= 4 * n, rolled[n], west)
        east = jnp.where((place >= 4 * n - 4) & (place < 12), rolled[n], east)
    return jnp.where(odd, west, east), jnp.where(odd, east, west)


def odd_lon():
    return lax.rem(lax.axis_index("lon"), 2) == 1


def main_slot():
    lat, lats, half = lax.axis_index("lat"), lax.axis_size("lat"), lax.axis_size("lon") // 2
    place = lax.rem(lax.axis_index("lon"), half)
    far = (lat == lats // 2 - 1) | (lat == lats // 2) | (lat == lats - 1)
    late = (place >= half - 2) & jnp.logical_not(far)
    return jnp.where((lat == lats - 2) & (place < 6), 0, jnp.where(late, 2, 1))


def pack_columns(fields, edges, part_b, part_a, rim):
    odd = odd_lon()
    tiles = []
    for i in range(CHUNKS):
        rows = pl.ds(8 * i, 8)
        tiles.append([edge_tile([fields[f][k, rows].astype(jnp.float32) for k in range(LEVELS)]) for f in range(5)])
    parts = [send_to(odd, row[:4]) for row in tiles]
    for j in range(CHUNKS // 4):
        parts.append(send_to(odd, [row[4] for row in tiles[4 * j : 4 * j + 4]]))
    for i, row in enumerate(tiles):
        for f in range(5):
            edges[f, 8 * i : 8 * i + 8] = row[f]
    for n, (to_a, to_b) in enumerate(parts):
        part_a[n] = to_a
        part_b[n] = to_b
    for f in range(5):
        for k in range(LEVELS):
            rim[f, k, 0:8] = fields[f][k, 0:8].astype(jnp.float32)
            rim[f, k, 8:16] = fields[f][k, ROWS - 8 : ROWS].astype(jnp.float32)


def mirrored(x):
    row = row_index()
    for bit in (1, 2):
        x = jnp.where((row & bit) == 0, row_roll(x, 8 - bit), row_roll(x, bit))
    flat = x.reshape(-1, LANES)
    back = LANES - 1 - lax.broadcasted_iota(jnp.int32, flat.shape, 1)
    return jnp.take_along_axis(flat, back, axis=1).reshape(x.shape)


def assemble_body(from_b, from_a, part_b, part_a, _, halo, edges, to_b, to_a):
    lat = lax.axis_index("lat")
    odd = lax.rem(lat, 2) == 1
    at_top = lat == lax.axis_size("lat") - 1
    upper = row_index() < 4
    pairs = 5 * LEVELS // 2

    def write(north, south):
        even = jnp.where(upper, north, row_roll(south, 4))
        other = jnp.where(upper, row_roll(north, 4), south)
        for n in range(pairs):
            f, m = divmod(n, LEVELS // 2)
            halo[f, 2 * m] = even[n]
            halo[f, 2 * m + 1] = other[n]

    @pl.when(at_top)
    def _():
        north = mirrored(from_b[...].reshape(pairs, 8, LANES))
        flip = LEVELS // 2 * 2
        north = jnp.concatenate([north[:flip], -north[flip : 2 * flip], north[2 * flip :]], axis=0)
        write(north, from_a[...].reshape(pairs, 8, LANES))

    @pl.when(jnp.logical_not(at_top))
    def _():
        a, b = from_a[...].reshape(pairs, 8, LANES), from_b[...].reshape(pairs, 8, LANES)
        write(jnp.where(odd, b, a), jnp.where(odd, a, b))

    tiles = []
    for f in range(5):
        tile = edge_tile([halo[f, k] for k in range(LEVELS)])
        edges[f] = tile
        tiles.append(tile)
    for part, out in ((part_a, to_a), (part_b, to_b)):
        for i in range(CHUNKS):
            out[i] = part[i]
        for j in range(CHUNKS // 4):
            out[CHUNKS + 1 + j] = part[CHUNKS + j]
    last = CHUNKS + 1 + CHUNKS // 4
    to_a[CHUNKS], to_b[CHUNKS] = send_to(odd_lon(), tiles[:4])
    to_a[last], to_b[last] = send_to(odd_lon(), tiles[4:])


def assemble(from_b, from_a, part_b, part_a, after):
    whole = jax.ShapeDtypeStruct((CHUNKS + 2 + CHUNKS // 4, 8, LANES), jnp.float32)
    return pl.pallas_call(
        assemble_body,
        out_shape=[
            jax.ShapeDtypeStruct((5, LEVELS, 8, LANES), jnp.float32),
            jax.ShapeDtypeStruct((5, 8, LANES), jnp.float32),
            whole,
            whole,
        ],
        compiler_params=pltpu.CompilerParams(vmem_limit_bytes=SMALL),
        name="assemble",
    )(from_b, from_a, part_b, part_a, after)


def step_scratch(levels, chunks):
    rows = 8 * chunks
    f32 = jnp.float32
    return [
        pltpu.VMEM((4, levels, rows + 8, LANES), f32),
        pltpu.VMEM((4, levels, rows + 8, LANES), f32),
        pltpu.VMEM((levels, rows + 8, LANES), f32),
        pltpu.VMEM((5, levels, rows, LANES), f32),
        pltpu.VMEM((5, levels, rows + 8, LANES), f32),
        pltpu.VMEM((levels, rows, LANES), f32),
        pltpu.VMEM((levels, rows, LANES), f32),
        pltpu.VMEM((levels, rows, LANES), f32),
        pltpu.VMEM((levels, rows, LANES), f32),
        pltpu.VMEM((levels, rows + 8, LANES), f32),
    ]


def pressure_by_level(rows, src):
    base = jnp.zeros((rows, LANES), jnp.float32)
    for k in range(LEVELS):
        h = density_tenth(src[0, k, 0:rows], src[1, k, 0:rows], (k + 0.5) / LEVELS)
        base = base + h
        yield base, lane_roll(base, -1)
        base = base + h


def run_substeps(
    levels, chunks, pressure, turn_rows, state_a, state_b, press, shifted, past, face_e, face_n, keep, turn, wet
):
    rows_all = 8 * chunks

    def load_faces(k, _):
        here = wet[k, 0:rows_all]
        face_e[k] = FACE * (here * lane_roll(here, -1))
        face_n[k] = FACE * (here * wet[k, 1 : rows_all + 1])
        keep[k] = 1.0 - DRAG * here
        turn[k] = here * turn_rows
        return 0

    lax.fori_loop(0, levels, load_faces, 0, unroll=True)

    def shift(src):
        for k, (base, ahead) in enumerate(pressure(rows_all, src)):
            press[k, 0:rows_all] = base
            for q in range(4):
                shifted[q, k] = lane_roll(src[q, k, 0:rows_all], -1)
            shifted[4, k] = ahead

    def update(src, dst, i, _):
        start = pl.multiple_of(8 * i, 8)
        rows, after = pl.ds(start, 8), pl.ds(start + 1, 8)
        for k in range(levels):
            now = [src[q, k, rows] for q in range(4)]
            p0 = press[k, rows]
            ahead = [shifted[q, k, rows] for q in range(5)]
            east = along_faces(face_e[k, rows], now, ahead[:4], 2, p0, ahead[4])
            west = [None if n == 3 else lane_roll(east[n], 1) for n in range(5)]
            nxt = [src[q, k, after] for q in range(4)]
            north = along_faces(face_n[k, rows], now, nxt, 3, p0, press[k, after])
            for n in (0, 1, 2, 4):
                past[n, k, pl.ds(start + 8, 8)] = north[n]
            south = [None if n == 3 else past[n, k, pl.ds(start + 7, 8)] for n in range(5)]
            new = combine(now, keep[k, rows], turn[k, rows], east, west, north, south)
            for q in range(4):
                dst[q, k, rows] = new[q]
        return 0

    def two_steps(half, _):
        shift(state_a)
        lax.fori_loop(0, chunks, functools.partial(update, state_a, state_b), 0, unroll=True)
        shift(state_b)
        lax.fori_loop(0, chunks, functools.partial(update, state_b, state_a), 0, unroll=True)
        return 0

    lax.fori_loop(0, NSUB // 2, two_steps, 0)


def held(f, x):
    return x * ASCALE if f in (2, 3) else x


def given(f, x):
    return x * (1.0 / ASCALE) if f in (2, 3) else x


def run_main(fields, outs, scratch):
    state, wet = scratch[0], scratch[-1]

    def load_in(k, _):
        for f in range(4):
            state[f, k, 0:ROWS] = held(f, fields[f][k])
        wet[k, 0:ROWS] = fields[4][k].astype(jnp.float32)
        return 0

    lax.fori_loop(0, LEVELS, load_in, 0, unroll=True)
    turn_rows = coriolis(lax.broadcasted_iota(jnp.int32, (ROWS, LANES), 0))
    run_substeps(LEVELS, CHUNKS, pressure_by_level, turn_rows, *scratch)

    def store_out(k, _):
        for f in range(4):
            outs[f, k] = given(f, state[f, k, 0:ROWS])
        return 0

    lax.fori_loop(0, LEVELS, store_out, 0, unroll=True)


def run_bands(rim, halo, out, scratch):
    state, wet = scratch[0], scratch[-1]

    def load_in(k, _):
        for f in range(4):
            state[f, k, 0:8] = held(f, rim[f, k, 8:16])
            state[f, k, 8:16] = held(f, halo[f, k])
            state[f, k, 16:24] = held(f, rim[f, k, 0:8])
        wet[k, 0:8] = rim[4, k, 8:16]
        wet[k, 8:16] = halo[4, k]
        wet[k, 16:24] = rim[4, k, 0:8]
        return 0

    lax.fori_loop(0, LEVELS, load_in, 0, unroll=True)
    place = lax.broadcasted_iota(jnp.int32, (24, LANES), 0)
    turn_rows = coriolis(jnp.where(place < 12, place + (ROWS - 8), place - 16))
    run_substeps(LEVELS, 3, pressure_by_level, turn_rows, *scratch)

    def store_out(k, _):
        for f in range(4):
            out[f, k, 0:8] = given(f, state[f, k, 16:24])
            out[f, k, 8:16] = given(f, state[f, k, 0:8])
        return 0

    lax.fori_loop(0, LEVELS, store_out, 0, unroll=True)


MAIN = jax.ShapeDtypeStruct((4, LEVELS, ROWS, LANES), jnp.float32)


def first_body(*refs):
    fields, (out, edges, part_b, part_a, rim, to_a), scratch = refs[:5], refs[5:11], refs[11:]
    pack_columns(fields, edges, part_b, part_a, rim)
    start = pl.multiple_of(jnp.where(odd_lat(), 0, 8), 8)
    pack_pairs(lambda f, k: rim[f, k, pl.ds(start, 8)], jnp.logical_not(odd_lat()), to_a)

    @pl.when(main_slot() == 0)
    def _():
        run_main(fields, out, scratch)


def first_block(fields):
    f32 = jnp.float32
    part = jax.ShapeDtypeStruct((CHUNKS + CHUNKS // 4, 8, LANES), f32)
    return pl.pallas_call(
        first_body,
        out_shape=[
            MAIN,
            jax.ShapeDtypeStruct((5, ROWS, LANES), f32),
            part,
            part,
            jax.ShapeDtypeStruct((5, LEVELS, 16, LANES), f32),
            jax.ShapeDtypeStruct((5, LEVELS // 2, 8, LANES), f32),
        ],
        scratch_shapes=step_scratch(LEVELS, CHUNKS),
        compiler_params=pltpu.CompilerParams(vmem_limit_bytes=VMEM),
        cost_estimate=pl.CostEstimate(flops=300_000_000, bytes_accessed=20_000_000, transcendentals=0),
        name="first_block",
    )(*fields)


def second_body(*refs):
    fields, (out, done), scratch = refs[:5], refs[6:8], refs[8:]
    done[...] = jnp.zeros_like(done)

    @pl.when(main_slot() == 1)
    def _():
        run_main(fields, out, scratch)


def second_block(fields, after):
    return pl.pallas_call(
        second_body,
        out_shape=[MAIN, jax.ShapeDtypeStruct((8, LANES), jnp.float32)],
        scratch_shapes=step_scratch(LEVELS, CHUNKS),
        compiler_params=pltpu.CompilerParams(vmem_limit_bytes=VMEM),
        cost_estimate=pl.CostEstimate(flops=300_000_000, bytes_accessed=20_000_000, transcendentals=0),
        name="second_block",
    )(*fields, after)


def third_body(*refs):
    fields, (rim, halo, out, band) = refs[:5], refs[5:9]
    main_scratch, band_scratch = refs[9:19], refs[19:]

    @pl.when(main_slot() == 2)
    def _():
        run_main(fields, out, main_scratch)

    run_bands(rim, halo, band, band_scratch)


def third_block(fields, rim, halo):
    return pl.pallas_call(
        third_body,
        out_shape=[MAIN, jax.ShapeDtypeStruct((4, LEVELS, 16, LANES), jnp.float32)],
        scratch_shapes=step_scratch(LEVELS, CHUNKS) + step_scratch(LEVELS, 3),
        compiler_params=pltpu.CompilerParams(vmem_limit_bytes=VMEM),
        cost_estimate=pl.CostEstimate(flops=200_000_000, bytes_accessed=10_000_000, transcendentals=0),
        name="third_block",
    )(*fields, rim, halo)


TALL = CHUNKS + 2


def pressure_by_lanes(rows, src):
    group = lax.broadcasted_iota(jnp.int32, (rows, LANES), 1) // 16
    depth = (group.astype(jnp.float32) + 0.5) / LEVELS
    source = lax.broadcasted_iota(jnp.int32, (LANES, 2 * LANES), 0)
    target = lax.broadcasted_iota(jnp.int32, (LANES, 2 * LANES), 1)
    target = jnp.where(target < LANES, target, (target - (LANES - 1)) % LANES)
    same = (source % 16) == (target % 16)
    weights = jnp.where(same & (source < target), 2.0, jnp.where(source == target, 1.0, 0.0))
    both = jnp.concatenate([density_tenth(src[0, t, 0:rows], src[1, t, 0:rows], depth) for t in range(2)], axis=0)
    pieces = []
    for _ in range(3):
        pieces.append(both.astype(jnp.bfloat16))
        both = both - pieces[-1].astype(jnp.float32)
    p = jnp.dot(jnp.concatenate(pieces, axis=0), weights.astype(jnp.bfloat16), preferred_element_type=jnp.float32)
    p = (p[4 * rows :] + p[2 * rows : 4 * rows]) + p[: 2 * rows]
    yield p[:rows, :LANES], p[:rows, LANES:]
    yield p[rows:, :LANES], p[rows:, LANES:]


def strips_body(edges, edge_halo, from_b, from_a, band, *refs):
    mains, outs, scratch = refs[:3], refs[3:7], refs[7:17]
    merged, sent = refs[17:]
    slot_now = jnp.full((8, LANES), main_slot())
    state, wet = scratch[0], scratch[-1]
    odd = odd_lon()
    lane = lane_index()
    place = lane % 16
    east_halo = (place >= 8) & (place < 12)
    west_halo = (place >= 4) & (place < 8)
    for i in range(CHUNKS + 1):
        for f in range(5):
            slot, chunk = (f, i) if f < 4 else (i % 4, CHUNKS + 1 + i // 4)
            own = edges[f, 8 * i : 8 * i + 8] if i < CHUNKS else edge_halo[f]
            a, b = from_a[chunk], from_b[chunk]
            east = jnp.where(east_halo, lane_roll(jnp.where(odd, b, a), 8 - 4 * slot), own)
            west = jnp.where(west_halo, lane_roll(jnp.where(odd, a, b), 8 - 4 * slot), own)
            for c in [1 + i] if i < CHUNKS else [0, CHUNKS + 1]:
                for t, tile in enumerate((east, west)):
                    if f < 4:
                        state[f, t, 8 * c : 8 * c + 8] = held(f, tile)
                    else:
                        wet[t, 8 * c : 8 * c + 8] = tile

    turn_rows = coriolis(lax.broadcasted_iota(jnp.int32, (8 * TALL, LANES), 0) - 8)
    run_substeps(2, TALL, pressure_by_lanes, turn_rows, *scratch)

    upper = row_index() < 4
    outer = (lane < 4) | (lane >= LANES - 4)
    copies = []
    for f in range(4):
        for i in range(CHUNKS):
            rows = pl.ds(8 * i, 8)
            c = 8 * (i + 1)
            edge = given(f, jnp.where(place < 8, state[f, 0, c : c + 8], state[f, 1, c : c + 8]))
            for k in range(LEVELS):
                block = jnp.where(slot_now == 1, mains[1][f, k, rows], mains[2][f, k, rows])
                block = jnp.where(slot_now == 0, mains[0][f, k, rows], block)
                if i == 0:
                    block = jnp.where(upper, band[f, k, 0:8], block)
                if i == CHUNKS - 1:
                    block = jnp.where(upper, block, band[f, k, 8:16])
                merged[f, k, rows] = jnp.where(outer, lane_roll(edge, -(16 * k + 8)), block)
        for n in range(2):
            half = pl.ds(n * LEVELS // 2, LEVELS // 2)
            copies.append(pltpu.make_async_copy(merged.at[f, half], outs[f].at[half], sent.at[2 * f + n]))
            copies[-1].start()
    for copy in copies:
        copy.wait()


def strips_and_merge(edges, edge_halo, from_b, from_a, band, mains):
    out = jax.ShapeDtypeStruct((LEVELS, ROWS, LANES), jnp.float32)
    return pl.pallas_call(
        strips_body,
        out_specs=[pl.BlockSpec(memory_space=pl.ANY)] * 4,
        out_shape=[out] * 4,
        scratch_shapes=step_scratch(2, TALL)
        + [pltpu.VMEM((4, LEVELS, ROWS, LANES), jnp.float32), pltpu.SemaphoreType.DMA((8,))],
        compiler_params=pltpu.CompilerParams(vmem_limit_bytes=VMEM),
        name="strips_and_merge",
    )(edges, edge_halo, from_b, from_a, band, *mains)


def lat_routes(lats, lons):
    first, second = [], []
    for j in range(lons):
        for i in range(lats):
            first.append((i * lons + j, (i ^ 1) * lons + j))
        for i in range(1, lats - 1):
            other = i + 1 if i % 2 else i - 1
            second.append((i * lons + j, other * lons + j))
        second.append(((lats - 1) * lons + j, (lats - 1) * lons + lons - 1 - j))
    return first, second


def lon_routes(lons):
    first = [(j, j ^ 1) for j in range(lons)]
    second = [(j, (j + 1 if j % 2 else j - 1) % lons) for j in range(lons)]
    return first, second


def on_device(*args):
    route_a, route_b = lat_routes(lax.axis_size("lat"), lax.axis_size("lon"))
    from_b = lax.ppermute(pack_rows(args), AXES, route_b)
    main_0, edges, part_b, part_a, rim, to_a = first_block(args)
    from_a = lax.ppermute(to_a, AXES, route_a)
    main_1, done = second_block(args, edges)
    halo, edge_halo, to_b, to_a = assemble(from_b, from_a, part_b, part_a, done)
    route_a, route_b = lon_routes(lax.axis_size("lon"))
    from_b = lax.ppermute(to_b, "lon", route_b)
    from_a = lax.ppermute(to_a, "lon", route_a)
    main_2, band = third_block(args, rim, halo)
    return tuple(strips_and_merge(edges, edge_halo, from_b, from_a, band, (main_0, main_1, main_2)))


def solution(mesh):
    spec = P(None, "lat", "lon")
    return jax.shard_map(
        on_device,
        mesh=mesh,
        in_specs=(spec,) * 5,
        out_specs=(spec,) * 4,
        check_vma=False,
    )
```

```python
import functools

import jax
import jax.numpy as jnp
from jax import lax
from jax.experimental import pallas as pl
from jax.experimental.pallas import tpu as pltpu
from jax.sharding import PartitionSpec as P

NSUB = 4
LEVELS = 8
ROWS = 64
LANES = 128
CHUNKS = ROWS // 8
AXES = ("lat", "lon")

FACE = 0.08
ASCALE = 0.0625 / 0.08
PSCALE = ASCALE * 0.15 / 0.08
DRAG = 0.05
VMEM = 24 * 1024 * 1024
SMALL = 4 * 1024 * 1024


def lane_roll(x, amount):
    amount %= LANES
    return x if amount == 0 else pltpu.roll(x, amount, axis=x.ndim - 1)


def row_roll(x, amount):
    return pltpu.roll(x, amount, axis=x.ndim - 2)


def lane_index(rows=8):
    return lax.broadcasted_iota(jnp.int32, (rows, LANES), 1)


def row_index():
    return lax.broadcasted_iota(jnp.int32, (8, LANES), 0)


def density_tenth(temper, salt, depth):
    c = PSCALE * 0.1
    return salt * (c * 0.8 + (c * 0.03) * temper) - temper * (
        (c * 0.25 + c * 0.1 * depth) + (c * 0.06) * temper
    )


def along_faces(k, now, nxt, normal, press_now, press_nxt):
    t0, s0, t1, s1 = now[0], now[1], nxt[0], nxt[1]
    a = now[normal] + nxt[normal]
    less = k * (1.0 - a)
    more = k * (1.0 + a)
    ft = less * t1 - more * t0
    fs = less * s1 - more * s0
    dn = nxt[normal] - now[normal]
    dp = press_nxt - press_now
    tang = 5 - normal
    ftang = k * (nxt[tang] - now[tang])
    ahead = k * (dn - dp)
    behind = k * (dn + dp)
    return ft, fs, ftang, ahead, behind


def combine(now, keep, turn, east, west, north, south):
    t, s, u, v = now
    nt = t + ((east[0] - west[0]) + (north[0] - south[0]))
    ns = s + ((east[1] - west[1]) + (north[1] - south[1]))
    nu = (keep * u + turn * v) + ((east[3] - west[4]) + (north[2] - south[2]))
    nv = (keep * v - turn * u) + ((east[2] - west[2]) + (north[3] - south[4]))
    return nt, ns, nu, nv


def coriolis(row):
    total = ROWS * lax.axis_size("lat")
    row = row + lax.axis_index("lat") * ROWS
    row = jnp.where(row >= total, 2 * total - 1 - row, row).astype(jnp.float32)
    return 0.1 + 0.3 * (row + 0.5) / total


def pack_pairs(take, top, out):
    upper = row_index() < 4
    for f in range(5):
        for m in range(LEVELS // 2):
            first, second = take(f, 2 * m), take(f, 2 * m + 1)
            lows = jnp.where(upper, first, row_roll(second, 4))
            highs = jnp.where(upper, row_roll(first, 4), second)
            out[f, m] = jnp.where(top, highs, lows)


def odd_lat():
    return lax.rem(lax.axis_index("lat"), 2) == 1


def pack_rows_body(*refs):
    fields, out, (held_rows, held_mask, arrived) = refs[:5], refs[5], refs[6:]
    start = pl.multiple_of(jnp.where(odd_lat(), ROWS - 8, 0), 8)
    copies = []
    for f in range(5):
        target = held_rows.at[f] if f < 4 else held_mask
        copies.append(pltpu.make_async_copy(fields[f].at[:, pl.ds(start, 8), :], target, arrived.at[f]))
    for copy in copies:
        copy.start()
    for copy in copies:
        copy.wait()
    pack_pairs(
        lambda f, k: held_rows[f, k] if f < 4 else held_mask[k].astype(jnp.float32), odd_lat(), out
    )


def pack_rows(fields):
    return pl.pallas_call(
        pack_rows_body,
        in_specs=[pl.BlockSpec(memory_space=pltpu.HBM)] * 5,
        out_specs=pl.BlockSpec(memory_space=pltpu.VMEM),
        out_shape=jax.ShapeDtypeStruct((5, LEVELS // 2, 8, LANES), jnp.float32),
        scratch_shapes=[
            pltpu.VMEM((4, LEVELS, 8, LANES), jnp.float32),
            pltpu.VMEM((LEVELS, 8, LANES), jnp.int32),
            pltpu.SemaphoreType.DMA((5,)),
        ],
        compiler_params=pltpu.CompilerParams(vmem_limit_bytes=SMALL),
        name="pack_rows",
    )(*[pltpu.with_memory_space_constraint(field, pltpu.HBM) for field in fields])


def edge_tile(levels):
    lane = lane_index()
    total = lane_roll(levels[0], 8)
    for k in range(1, LEVELS):
        total = jnp.where(lane >= 16 * k, lane_roll(levels[k], 16 * k + 8), total)
    return total


def send_to(odd, tiles):
    place = lane_index() % 16
    rolled = [lane_roll(tile, 4 * n - 8) for n, tile in enumerate(tiles)]
    west = east = rolled[0]
    for n in range(1, len(tiles)):
        west = jnp.where(place >= 4 * n, rolled[n], west)
        east = jnp.where((place >= 4 * n - 4) & (place < 12), rolled[n], east)
    return jnp.where(odd, west, east), jnp.where(odd, east, west)


def odd_lon():
    return lax.rem(lax.axis_index("lon"), 2) == 1


def main_slot():
    lat, lats, half = lax.axis_index("lat"), lax.axis_size("lat"), lax.axis_size("lon") // 2
    place = lax.rem(lax.axis_index("lon"), half)
    far = (lat == lats // 2 - 1) | (lat == lats // 2) | (lat == lats - 1)
    late = (place >= half - 2) & jnp.logical_not(far)
    return jnp.where((lat == lats - 2) & (place < 6), 0, jnp.where(late, 2, 1))


def pack_columns(fields, edges, part_b, part_a, rim):
    odd = odd_lon()
    tiles = []
    for i in range(CHUNKS):
        rows = pl.ds(8 * i, 8)
        tiles.append([edge_tile([fields[f][k, rows].astype(jnp.float32) for k in range(LEVELS)]) for f in range(5)])
    parts = [send_to(odd, row[:4]) for row in tiles]
    for j in range(CHUNKS // 4):
        parts.append(send_to(odd, [row[4] for row in tiles[4 * j : 4 * j + 4]]))
    for i, row in enumerate(tiles):
        for f in range(5):
            edges[f, 8 * i : 8 * i + 8] = row[f]
    for n, (to_a, to_b) in enumerate(parts):
        part_a[n] = to_a
        part_b[n] = to_b
    for f in range(5):
        for k in range(LEVELS):
            rim[f, k, 0:8] = fields[f][k, 0:8].astype(jnp.float32)
            rim[f, k, 8:16] = fields[f][k, ROWS - 8 : ROWS].astype(jnp.float32)


def mirrored(x):
    row = row_index()
    for bit in (1, 2):
        x = jnp.where((row & bit) == 0, row_roll(x, 8 - bit), row_roll(x, bit))
    flat = x.reshape(-1, LANES)
    back = LANES - 1 - lax.broadcasted_iota(jnp.int32, flat.shape, 1)
    return jnp.take_along_axis(flat, back, axis=1).reshape(x.shape)


def assemble_body(from_b, from_a, part_b, part_a, _, halo, edges, to_b, to_a):
    lat = lax.axis_index("lat")
    odd = lax.rem(lat, 2) == 1
    at_top = lat == lax.axis_size("lat") - 1
    upper = row_index() < 4
    pairs = 5 * LEVELS // 2

    def write(north, south):
        even = jnp.where(upper, north, row_roll(south, 4))
        other = jnp.where(upper, row_roll(north, 4), south)
        for n in range(pairs):
            f, m = divmod(n, LEVELS // 2)
            halo[f, 2 * m] = even[n]
            halo[f, 2 * m + 1] = other[n]

    @pl.when(at_top)
    def _():
        north = mirrored(from_b[...].reshape(pairs, 8, LANES))
        flip = LEVELS // 2 * 2
        north = jnp.concatenate([north[:flip], -north[flip : 2 * flip], north[2 * flip :]], axis=0)
        write(north, from_a[...].reshape(pairs, 8, LANES))

    @pl.when(jnp.logical_not(at_top))
    def _():
        a, b = from_a[...].reshape(pairs, 8, LANES), from_b[...].reshape(pairs, 8, LANES)
        write(jnp.where(odd, b, a), jnp.where(odd, a, b))

    tiles = []
    for f in range(5):
        tile = edge_tile([halo[f, k] for k in range(LEVELS)])
        edges[f] = tile
        tiles.append(tile)
    for part, out in ((part_a, to_a), (part_b, to_b)):
        for i in range(CHUNKS):
            out[i] = part[i]
        for j in range(CHUNKS // 4):
            out[CHUNKS + 1 + j] = part[CHUNKS + j]
    last = CHUNKS + 1 + CHUNKS // 4
    to_a[CHUNKS], to_b[CHUNKS] = send_to(odd_lon(), tiles[:4])
    to_a[last], to_b[last] = send_to(odd_lon(), tiles[4:])


def assemble(from_b, from_a, part_b, part_a, after):
    whole = jax.ShapeDtypeStruct((CHUNKS + 2 + CHUNKS // 4, 8, LANES), jnp.float32)
    return pl.pallas_call(
        assemble_body,
        out_shape=[
            jax.ShapeDtypeStruct((5, LEVELS, 8, LANES), jnp.float32),
            jax.ShapeDtypeStruct((5, 8, LANES), jnp.float32),
            whole,
            whole,
        ],
        compiler_params=pltpu.CompilerParams(vmem_limit_bytes=SMALL),
        name="assemble",
    )(from_b, from_a, part_b, part_a, after)


def step_scratch(levels, chunks):
    rows = 8 * chunks
    f32 = jnp.float32
    return [
        pltpu.VMEM((4, levels, rows + 8, LANES), f32),
        pltpu.VMEM((4, levels, rows + 8, LANES), f32),
        pltpu.VMEM((levels, rows + 8, LANES), f32),
        pltpu.VMEM((5, levels, rows, LANES), f32),
        pltpu.VMEM((5, levels, rows + 8, LANES), f32),
        pltpu.VMEM((levels, rows, LANES), f32),
        pltpu.VMEM((levels, rows, LANES), f32),
        pltpu.VMEM((levels, rows, LANES), f32),
        pltpu.VMEM((levels, rows, LANES), f32),
        pltpu.VMEM((levels, rows + 8, LANES), f32),
    ]


def pressure_by_level(rows, src):
    base = jnp.zeros((rows, LANES), jnp.float32)
    for k in range(LEVELS):
        h = density_tenth(src[0, k, 0:rows], src[1, k, 0:rows], (k + 0.5) / LEVELS)
        base = base + h
        yield base, lane_roll(base, -1)
        base = base + h


def run_substeps(
    levels, chunks, pressure, turn_rows, state_a, state_b, press, shifted, past, face_e, face_n, keep, turn, wet
):
    rows_all = 8 * chunks

    def load_faces(k, _):
        here = wet[k, 0:rows_all]
        face_e[k] = FACE * (here * lane_roll(here, -1))
        face_n[k] = FACE * (here * wet[k, 1 : rows_all + 1])
        keep[k] = 1.0 - DRAG * here
        turn[k] = here * turn_rows
        return 0

    lax.fori_loop(0, levels, load_faces, 0, unroll=True)

    def shift(src):
        for k, (base, ahead) in enumerate(pressure(rows_all, src)):
            press[k, 0:rows_all] = base
            for q in range(4):
                shifted[q, k] = lane_roll(src[q, k, 0:rows_all], -1)
            shifted[4, k] = ahead

    first_row = row_index() == 0

    def update(src, dst, i, _, before=None):
        start = 8 * i if isinstance(i, int) else pl.multiple_of(8 * i, 8)
        rows, after = pl.ds(start, 8), pl.ds(start + 1, 8)
        for k in range(levels):
            now = [src[q, k, rows] for q in range(4)]
            p0 = press[k, rows]
            ahead = [shifted[q, k, rows] for q in range(5)]
            east = along_faces(face_e[k, rows], now, ahead[:4], 2, p0, ahead[4])
            west = [None if n == 3 else lane_roll(east[n], 1) for n in range(5)]
            nxt = [src[q, k, after] for q in range(4)]
            north = along_faces(face_n[k, rows], now, nxt, 3, p0, press[k, after])
            if before is None:
                for n in (0, 1, 2, 4):
                    past[n, k, pl.ds(start + 8, 8)] = north[n]
                south = [None if n == 3 else past[n, k, pl.ds(start + 7, 8)] for n in range(5)]
            else:
                moved = [None if n == 3 else row_roll(north[n], 1) for n in range(5)]
                held_over = before.get(k, moved)
                south = [None if n == 3 else jnp.where(first_row, held_over[n], moved[n]) for n in range(5)]
                before[k] = moved
            new = combine(now, keep[k, rows], turn[k, rows], east, west, north, south)
            for q in range(4):
                dst[q, k, rows] = new[q]
        return 0

    def two_steps(half, _):
        shift(state_a)
        if levels == 2:
            before = {}
            for i in range(chunks):
                update(state_a, state_b, i, 0, before)
        else:
            lax.fori_loop(0, chunks, functools.partial(update, state_a, state_b), 0, unroll=True)
        shift(state_b)
        if levels == 2:
            before = {}
            for i in range(chunks):
                update(state_b, state_a, i, 0, before)
        else:
            lax.fori_loop(0, chunks, functools.partial(update, state_b, state_a), 0, unroll=True)
        return 0

    lax.fori_loop(0, NSUB // 2, two_steps, 0)


def held(f, x):
    return x * ASCALE if f in (2, 3) else x


def given(f, x):
    return x * (1.0 / ASCALE) if f in (2, 3) else x


def run_main(fields, outs, scratch):
    state, wet = scratch[0], scratch[-1]

    def load_in(k, _):
        for f in range(4):
            state[f, k, 0:ROWS] = held(f, fields[f][k])
        wet[k, 0:ROWS] = fields[4][k].astype(jnp.float32)
        return 0

    lax.fori_loop(0, LEVELS, load_in, 0, unroll=True)
    turn_rows = coriolis(lax.broadcasted_iota(jnp.int32, (ROWS, LANES), 0))
    run_substeps(LEVELS, CHUNKS, pressure_by_level, turn_rows, *scratch)

    def store_out(k, _):
        for f in range(4):
            outs[f, k] = given(f, state[f, k, 0:ROWS])
        return 0

    lax.fori_loop(0, LEVELS, store_out, 0, unroll=True)


def run_bands(rim, halo, out, scratch):
    state, wet = scratch[0], scratch[-1]

    def load_in(k, _):
        for f in range(4):
            state[f, k, 0:8] = held(f, rim[f, k, 8:16])
            state[f, k, 8:16] = held(f, halo[f, k])
            state[f, k, 16:24] = held(f, rim[f, k, 0:8])
        wet[k, 0:8] = rim[4, k, 8:16]
        wet[k, 8:16] = halo[4, k]
        wet[k, 16:24] = rim[4, k, 0:8]
        return 0

    lax.fori_loop(0, LEVELS, load_in, 0, unroll=True)
    place = lax.broadcasted_iota(jnp.int32, (24, LANES), 0)
    turn_rows = coriolis(jnp.where(place < 12, place + (ROWS - 8), place - 16))
    run_substeps(LEVELS, 3, pressure_by_level, turn_rows, *scratch)

    def store_out(k, _):
        for f in range(4):
            out[f, k, 0:8] = given(f, state[f, k, 16:24])
            out[f, k, 8:16] = given(f, state[f, k, 0:8])
        return 0

    lax.fori_loop(0, LEVELS, store_out, 0, unroll=True)


MAIN = jax.ShapeDtypeStruct((4, LEVELS, ROWS, LANES), jnp.float32)


def first_body(*refs):
    fields, (out, edges, part_b, part_a, rim, to_a), scratch = refs[:5], refs[5:11], refs[11:]
    pack_columns(fields, edges, part_b, part_a, rim)
    start = pl.multiple_of(jnp.where(odd_lat(), 0, 8), 8)
    pack_pairs(lambda f, k: rim[f, k, pl.ds(start, 8)], jnp.logical_not(odd_lat()), to_a)

    @pl.when(main_slot() == 0)
    def _():
        run_main(fields, out, scratch)


def first_block(fields):
    f32 = jnp.float32
    part = jax.ShapeDtypeStruct((CHUNKS + CHUNKS // 4, 8, LANES), f32)
    return pl.pallas_call(
        first_body,
        out_shape=[
            MAIN,
            jax.ShapeDtypeStruct((5, ROWS, LANES), f32),
            part,
            part,
            jax.ShapeDtypeStruct((5, LEVELS, 16, LANES), f32),
            jax.ShapeDtypeStruct((5, LEVELS // 2, 8, LANES), f32),
        ],
        scratch_shapes=step_scratch(LEVELS, CHUNKS),
        compiler_params=pltpu.CompilerParams(vmem_limit_bytes=VMEM),
        cost_estimate=pl.CostEstimate(flops=300_000_000, bytes_accessed=20_000_000, transcendentals=0),
        name="first_block",
    )(*fields)


def second_body(*refs):
    fields, (out, done), scratch = refs[:5], refs[6:8], refs[8:]
    done[...] = jnp.zeros_like(done)

    @pl.when(main_slot() == 1)
    def _():
        run_main(fields, out, scratch)


def second_block(fields, after):
    return pl.pallas_call(
        second_body,
        out_shape=[MAIN, jax.ShapeDtypeStruct((8, LANES), jnp.float32)],
        scratch_shapes=step_scratch(LEVELS, CHUNKS),
        compiler_params=pltpu.CompilerParams(vmem_limit_bytes=VMEM),
        cost_estimate=pl.CostEstimate(flops=300_000_000, bytes_accessed=20_000_000, transcendentals=0),
        name="second_block",
    )(*fields, after)


def third_body(*refs):
    fields, (rim, halo, out, band) = refs[:5], refs[5:9]
    main_scratch, band_scratch = refs[9:19], refs[19:]

    @pl.when(main_slot() == 2)
    def _():
        run_main(fields, out, main_scratch)

    run_bands(rim, halo, band, band_scratch)


def third_block(fields, rim, halo):
    return pl.pallas_call(
        third_body,
        out_shape=[MAIN, jax.ShapeDtypeStruct((4, LEVELS, 16, LANES), jnp.float32)],
        scratch_shapes=step_scratch(LEVELS, CHUNKS) + step_scratch(LEVELS, 3),
        compiler_params=pltpu.CompilerParams(vmem_limit_bytes=VMEM),
        cost_estimate=pl.CostEstimate(flops=200_000_000, bytes_accessed=10_000_000, transcendentals=0),
        name="third_block",
    )(*fields, rim, halo)


TALL = CHUNKS + 2


def pressure_by_lanes(rows, src):
    group = lax.broadcasted_iota(jnp.int32, (rows, LANES), 1) // 16
    depth = (group.astype(jnp.float32) + 0.5) / LEVELS
    source = lax.broadcasted_iota(jnp.int32, (LANES, 2 * LANES), 0)
    target = lax.broadcasted_iota(jnp.int32, (LANES, 2 * LANES), 1)
    target = jnp.where(target < LANES, target, (target - (LANES - 1)) % LANES)
    same = (source % 16) == (target % 16)
    weights = jnp.where(same & (source < target), 2.0, jnp.where(source == target, 1.0, 0.0))
    both = jnp.concatenate([density_tenth(src[0, t, 0:rows], src[1, t, 0:rows], depth) for t in range(2)], axis=0)
    pieces = []
    for _ in range(3):
        pieces.append(both.astype(jnp.bfloat16))
        both = both - pieces[-1].astype(jnp.float32)
    p = jnp.dot(jnp.concatenate(pieces, axis=0), weights.astype(jnp.bfloat16), preferred_element_type=jnp.float32)
    p = (p[4 * rows :] + p[2 * rows : 4 * rows]) + p[: 2 * rows]
    yield p[:rows, :LANES], p[:rows, LANES:]
    yield p[rows:, :LANES], p[rows:, LANES:]


def strips_body(edges, edge_halo, from_b, from_a, band, *refs):
    mains, outs, scratch = refs[:3], refs[3:7], refs[7:17]
    merged, sent = refs[17:]
    slot_now = jnp.full((8, LANES), main_slot())
    state, wet = scratch[0], scratch[-1]
    odd = odd_lon()
    lane = lane_index()
    place = lane % 16
    east_halo = (place >= 8) & (place < 12)
    west_halo = (place >= 4) & (place < 8)
    for i in range(CHUNKS + 1):
        for f in range(5):
            slot, chunk = (f, i) if f < 4 else (i % 4, CHUNKS + 1 + i // 4)
            own = edges[f, 8 * i : 8 * i + 8] if i < CHUNKS else edge_halo[f]
            a, b = from_a[chunk], from_b[chunk]
            east = jnp.where(east_halo, lane_roll(jnp.where(odd, b, a), 8 - 4 * slot), own)
            west = jnp.where(west_halo, lane_roll(jnp.where(odd, a, b), 8 - 4 * slot), own)
            for c in [1 + i] if i < CHUNKS else [0, CHUNKS + 1]:
                for t, tile in enumerate((east, west)):
                    if f < 4:
                        state[f, t, 8 * c : 8 * c + 8] = held(f, tile)
                    else:
                        wet[t, 8 * c : 8 * c + 8] = tile

    turn_rows = coriolis(lax.broadcasted_iota(jnp.int32, (8 * TALL, LANES), 0) - 8)
    run_substeps(2, TALL, pressure_by_lanes, turn_rows, *scratch)

    upper = row_index() < 4
    outer = (lane < 4) | (lane >= LANES - 4)
    copies = []
    for f in range(4):
        tiles = []
        for i in range(CHUNKS):
            c = 8 * (i + 1)
            tiles.append(given(f, jnp.where(place < 8, state[f, 0, c : c + 8], state[f, 1, c : c + 8])))
        for n in range(2):
            for i in range(CHUNKS):
                rows = pl.ds(8 * i, 8)
                for k in range(n * LEVELS // 2, (n + 1) * LEVELS // 2):
                    block = jnp.where(slot_now == 1, mains[1][f, k, rows], mains[2][f, k, rows])
                    block = jnp.where(slot_now == 0, mains[0][f, k, rows], block)
                    if i == 0:
                        block = jnp.where(upper, band[f, k, 0:8], block)
                    if i == CHUNKS - 1:
                        block = jnp.where(upper, block, band[f, k, 8:16])
                    merged[f, k, rows] = jnp.where(outer, lane_roll(tiles[i], -(16 * k + 8)), block)
            half = pl.ds(n * LEVELS // 2, LEVELS // 2)
            copies.append(pltpu.make_async_copy(merged.at[f, half], outs[f].at[half], sent.at[2 * f + n]))
            copies[-1].start()
    for copy in copies:
        copy.wait()


def strips_and_merge(edges, edge_halo, from_b, from_a, band, mains):
    out = jax.ShapeDtypeStruct((LEVELS, ROWS, LANES), jnp.float32)
    return pl.pallas_call(
        strips_body,
        out_specs=[pl.BlockSpec(memory_space=pl.ANY)] * 4,
        out_shape=[out] * 4,
        scratch_shapes=step_scratch(2, TALL)
        + [pltpu.VMEM((4, LEVELS, ROWS, LANES), jnp.float32), pltpu.SemaphoreType.DMA((8,))],
        compiler_params=pltpu.CompilerParams(vmem_limit_bytes=VMEM),
        name="strips_and_merge",
    )(edges, edge_halo, from_b, from_a, band, *mains)


def lat_routes(lats, lons):
    first, second = [], []
    for j in range(lons):
        for i in range(lats):
            first.append((i * lons + j, (i ^ 1) * lons + j))
        for i in range(1, lats - 1):
            other = i + 1 if i % 2 else i - 1
            second.append((i * lons + j, other * lons + j))
        second.append(((lats - 1) * lons + j, (lats - 1) * lons + lons - 1 - j))
    return first, second


def lon_routes(lons):
    first = [(j, j ^ 1) for j in range(lons)]
    second = [(j, (j + 1 if j % 2 else j - 1) % lons) for j in range(lons)]
    return first, second


def on_device(*args):
    route_a, route_b = lat_routes(lax.axis_size("lat"), lax.axis_size("lon"))
    from_b = lax.ppermute(pack_rows(args), AXES, route_b)
    main_0, edges, part_b, part_a, rim, to_a = first_block(args)
    from_a = lax.ppermute(to_a, AXES, route_a)
    main_1, done = second_block(args, edges)
    halo, edge_halo, to_b, to_a = assemble(from_b, from_a, part_b, part_a, done)
    route_a, route_b = lon_routes(lax.axis_size("lon"))
    from_b = lax.ppermute(to_b, "lon", route_b)
    from_a = lax.ppermute(to_a, "lon", route_a)
    main_2, band = third_block(args, rim, halo)
    return tuple(strips_and_merge(edges, edge_halo, from_b, from_a, band, (main_0, main_1, main_2)))


def solution(mesh):
    spec = P(None, "lat", "lon")
    return jax.shard_map(
        on_device,
        mesh=mesh,
        in_specs=(spec,) * 5,
        out_specs=(spec,) * 4,
        check_vma=False,
    )
```

```python
import functools

import jax
import jax.numpy as jnp
from jax import lax
from jax.experimental import pallas as pl
from jax.experimental.pallas import tpu as pltpu
from jax.sharding import PartitionSpec as P

NSUB = 4
LEVELS = 8
ROWS = 64
LANES = 128
CHUNKS = ROWS // 8
AXES = ("lat", "lon")

FACE = 0.08
ASCALE = 0.0625 / 0.08
PSCALE = ASCALE * 0.15 / 0.08
DRAG = 0.05
VMEM = 24 * 1024 * 1024
SMALL = 4 * 1024 * 1024


def lane_roll(x, amount):
    amount %= LANES
    return x if amount == 0 else pltpu.roll(x, amount, axis=x.ndim - 1)


def row_roll(x, amount):
    return pltpu.roll(x, amount, axis=x.ndim - 2)


def lane_index(rows=8):
    return lax.broadcasted_iota(jnp.int32, (rows, LANES), 1)


def row_index():
    return lax.broadcasted_iota(jnp.int32, (8, LANES), 0)


def density_tenth(temper, salt, depth):
    c = PSCALE * 0.1
    return salt * (c * 0.8 + (c * 0.03) * temper) - temper * (
        (c * 0.25 + c * 0.1 * depth) + (c * 0.06) * temper
    )


def along_faces(k, now, nxt, normal, press_now, press_nxt):
    t0, s0, t1, s1 = now[0], now[1], nxt[0], nxt[1]
    a = now[normal] + nxt[normal]
    less = k * (1.0 - a)
    more = k * (1.0 + a)
    ft = less * t1 - more * t0
    fs = less * s1 - more * s0
    dn = nxt[normal] - now[normal]
    dp = press_nxt - press_now
    tang = 5 - normal
    ftang = k * (nxt[tang] - now[tang])
    ahead = k * (dn - dp)
    behind = k * (dn + dp)
    return ft, fs, ftang, ahead, behind


def combine(now, keep, turn, east, west, north, south):
    t, s, u, v = now
    nt = t + ((east[0] - west[0]) + (north[0] - south[0]))
    ns = s + ((east[1] - west[1]) + (north[1] - south[1]))
    nu = (keep * u + turn * v) + ((east[3] - west[4]) + (north[2] - south[2]))
    nv = (keep * v - turn * u) + ((east[2] - west[2]) + (north[3] - south[4]))
    return nt, ns, nu, nv


def coriolis(row):
    total = ROWS * lax.axis_size("lat")
    row = row + lax.axis_index("lat") * ROWS
    row = jnp.where(row >= total, 2 * total - 1 - row, row).astype(jnp.float32)
    return 0.1 + 0.3 * (row + 0.5) / total


def pack_pairs(take, top, out):
    upper = row_index() < 4
    for f in range(5):
        for m in range(LEVELS // 2):
            first, second = take(f, 2 * m), take(f, 2 * m + 1)
            lows = jnp.where(upper, first, row_roll(second, 4))
            highs = jnp.where(upper, row_roll(first, 4), second)
            out[f, m] = jnp.where(top, highs, lows)


def odd_lat():
    return lax.rem(lax.axis_index("lat"), 2) == 1


def pack_rows_body(*refs):
    fields, out, (held_rows, held_mask, arrived) = refs[:5], refs[5], refs[6:]
    start = pl.multiple_of(jnp.where(odd_lat(), ROWS - 8, 0), 8)
    copies = []
    for f in range(5):
        target = held_rows.at[f] if f < 4 else held_mask
        copies.append(pltpu.make_async_copy(fields[f].at[:, pl.ds(start, 8), :], target, arrived.at[f]))
    for copy in copies:
        copy.start()

    def take(f, k):
        if k == 0:
            copies[f].wait()
        return held_rows[f, k] if f < 4 else held_mask[k].astype(jnp.float32)

    pack_pairs(take, odd_lat(), out)


def pack_rows(fields):
    return pl.pallas_call(
        pack_rows_body,
        in_specs=[pl.BlockSpec(memory_space=pltpu.HBM)] * 5,
        out_specs=pl.BlockSpec(memory_space=pltpu.VMEM),
        out_shape=jax.ShapeDtypeStruct((5, LEVELS // 2, 8, LANES), jnp.float32),
        scratch_shapes=[
            pltpu.VMEM((4, LEVELS, 8, LANES), jnp.float32),
            pltpu.VMEM((LEVELS, 8, LANES), jnp.int32),
            pltpu.SemaphoreType.DMA((5,)),
        ],
        compiler_params=pltpu.CompilerParams(vmem_limit_bytes=SMALL),
        name="pack_rows",
    )(*[pltpu.with_memory_space_constraint(field, pltpu.HBM) for field in fields])


def edge_tile(levels):
    lane = lane_index()
    total = lane_roll(levels[0], 8)
    for k in range(1, LEVELS):
        total = jnp.where(lane >= 16 * k, lane_roll(levels[k], 16 * k + 8), total)
    return total


def send_to(odd, tiles):
    place = lane_index() % 16
    rolled = [lane_roll(tile, 4 * n - 8) for n, tile in enumerate(tiles)]
    west = east = rolled[0]
    for n in range(1, len(tiles)):
        west = jnp.where(place >= 4 * n, rolled[n], west)
        east = jnp.where((place >= 4 * n - 4) & (place < 12), rolled[n], east)
    return jnp.where(odd, west, east), jnp.where(odd, east, west)


def odd_lon():
    return lax.rem(lax.axis_index("lon"), 2) == 1


def main_slot():
    lat, lats, half = lax.axis_index("lat"), lax.axis_size("lat"), lax.axis_size("lon") // 2
    place = lax.rem(lax.axis_index("lon"), half)
    far = (lat == lats // 2 - 1) | (lat == lats // 2) | (lat == lats - 1)
    late = (place >= half - 2) & jnp.logical_not(far)
    return jnp.where((lat == lats - 2) & (place < 6), 0, jnp.where(late, 2, 1))


def pack_columns(fields, edges, part_b, part_a, rim):
    odd = odd_lon()
    tiles = []
    for i in range(CHUNKS):
        rows = pl.ds(8 * i, 8)
        tiles.append([edge_tile([fields[f][k, rows].astype(jnp.float32) for k in range(LEVELS)]) for f in range(5)])
    parts = [send_to(odd, row[:4]) for row in tiles]
    for j in range(CHUNKS // 4):
        parts.append(send_to(odd, [row[4] for row in tiles[4 * j : 4 * j + 4]]))
    for i, row in enumerate(tiles):
        for f in range(5):
            edges[f, 8 * i : 8 * i + 8] = row[f]
    for n, (to_a, to_b) in enumerate(parts):
        part_a[n] = to_a
        part_b[n] = to_b
    for f in range(5):
        for k in range(LEVELS):
            rim[f, k, 0:8] = fields[f][k, 0:8].astype(jnp.float32)
            rim[f, k, 8:16] = fields[f][k, ROWS - 8 : ROWS].astype(jnp.float32)


def mirrored(x):
    row = row_index()
    for bit in (1, 2):
        x = jnp.where((row & bit) == 0, row_roll(x, 8 - bit), row_roll(x, bit))
    flat = x.reshape(-1, LANES)
    back = LANES - 1 - lax.broadcasted_iota(jnp.int32, flat.shape, 1)
    return jnp.take_along_axis(flat, back, axis=1).reshape(x.shape)


def assemble_body(from_b, from_a, part_b, part_a, _, halo, edges, to_b, to_a):
    lat = lax.axis_index("lat")
    odd = lax.rem(lat, 2) == 1
    at_top = lat == lax.axis_size("lat") - 1
    upper = row_index() < 4
    pairs = 5 * LEVELS // 2

    def write(north, south):
        even = jnp.where(upper, north, row_roll(south, 4))
        other = jnp.where(upper, row_roll(north, 4), south)
        for n in range(pairs):
            f, m = divmod(n, LEVELS // 2)
            halo[f, 2 * m] = even[n]
            halo[f, 2 * m + 1] = other[n]

    @pl.when(at_top)
    def _():
        north = mirrored(from_b[...].reshape(pairs, 8, LANES))
        flip = LEVELS // 2 * 2
        north = jnp.concatenate([north[:flip], -north[flip : 2 * flip], north[2 * flip :]], axis=0)
        write(north, from_a[...].reshape(pairs, 8, LANES))

    @pl.when(jnp.logical_not(at_top))
    def _():
        a, b = from_a[...].reshape(pairs, 8, LANES), from_b[...].reshape(pairs, 8, LANES)
        write(jnp.where(odd, b, a), jnp.where(odd, a, b))

    tiles = []
    for f in range(5):
        tile = edge_tile([halo[f, k] for k in range(LEVELS)])
        edges[f] = tile
        tiles.append(tile)
    for part, out in ((part_a, to_a), (part_b, to_b)):
        for i in range(CHUNKS):
            out[i] = part[i]
        for j in range(CHUNKS // 4):
            out[CHUNKS + 1 + j] = part[CHUNKS + j]
    last = CHUNKS + 1 + CHUNKS // 4
    to_a[CHUNKS], to_b[CHUNKS] = send_to(odd_lon(), tiles[:4])
    to_a[last], to_b[last] = send_to(odd_lon(), tiles[4:])


def assemble(from_b, from_a, part_b, part_a, after):
    whole = jax.ShapeDtypeStruct((CHUNKS + 2 + CHUNKS // 4, 8, LANES), jnp.float32)
    return pl.pallas_call(
        assemble_body,
        out_shape=[
            jax.ShapeDtypeStruct((5, LEVELS, 8, LANES), jnp.float32),
            jax.ShapeDtypeStruct((5, 8, LANES), jnp.float32),
            whole,
            whole,
        ],
        compiler_params=pltpu.CompilerParams(vmem_limit_bytes=SMALL),
        name="assemble",
    )(from_b, from_a, part_b, part_a, after)


def step_scratch(levels, chunks):
    rows = 8 * chunks
    f32 = jnp.float32
    return [
        pltpu.VMEM((4, levels, rows + 8, LANES), f32),
        pltpu.VMEM((4, levels, rows + 8, LANES), f32),
        pltpu.VMEM((levels, rows + 8, LANES), f32),
        pltpu.VMEM((5, levels, rows, LANES), f32),
        pltpu.VMEM((5, levels, rows + 8, LANES), f32),
        pltpu.VMEM((levels, rows, LANES), f32),
        pltpu.VMEM((levels, rows, LANES), f32),
        pltpu.VMEM((levels, rows, LANES), f32),
        pltpu.VMEM((levels, rows, LANES), f32),
        pltpu.VMEM((levels, rows + 8, LANES), f32),
    ]


def pressure_by_level(rows, src):
    base = jnp.zeros((rows, LANES), jnp.float32)
    for k in range(LEVELS):
        h = density_tenth(src[0, k, 0:rows], src[1, k, 0:rows], (k + 0.5) / LEVELS)
        base = base + h
        yield base, lane_roll(base, -1)
        base = base + h


def run_substeps(
    levels, chunks, pressure, turn_rows, state_a, state_b, press, shifted, past, face_e, face_n, keep, turn, wet
):
    rows_all = 8 * chunks

    def load_faces(k, _):
        here = wet[k, 0:rows_all]
        face_e[k] = FACE * (here * lane_roll(here, -1))
        face_n[k] = FACE * (here * wet[k, 1 : rows_all + 1])
        keep[k] = 1.0 - DRAG * here
        turn[k] = here * turn_rows
        return 0

    lax.fori_loop(0, levels, load_faces, 0, unroll=True)

    def shift(src):
        for k, (base, ahead) in enumerate(pressure(rows_all, src)):
            press[k, 0:rows_all] = base
            for q in range(4):
                shifted[q, k] = lane_roll(src[q, k, 0:rows_all], -1)
            shifted[4, k] = ahead

    def update(src, dst, i, _):
        start = pl.multiple_of(8 * i, 8)
        rows, after = pl.ds(start, 8), pl.ds(start + 1, 8)
        for k in range(levels):
            now = [src[q, k, rows] for q in range(4)]
            p0 = press[k, rows]
            ahead = [shifted[q, k, rows] for q in range(5)]
            east = along_faces(face_e[k, rows], now, ahead[:4], 2, p0, ahead[4])
            west = [None if n == 3 else lane_roll(east[n], 1) for n in range(5)]
            nxt = [src[q, k, after] for q in range(4)]
            north = along_faces(face_n[k, rows], now, nxt, 3, p0, press[k, after])
            for n in (0, 1, 2, 4):
                past[n, k, pl.ds(start + 8, 8)] = north[n]
            south = [None if n == 3 else past[n, k, pl.ds(start + 7, 8)] for n in range(5)]
            new = combine(now, keep[k, rows], turn[k, rows], east, west, north, south)
            for q in range(4):
                dst[q, k, rows] = new[q]
        return 0

    def two_steps(half, _):
        shift(state_a)
        lax.fori_loop(0, chunks, functools.partial(update, state_a, state_b), 0, unroll=True)
        shift(state_b)
        lax.fori_loop(0, chunks, functools.partial(update, state_b, state_a), 0, unroll=True)
        return 0

    lax.fori_loop(0, NSUB // 2, two_steps, 0)


def held(f, x):
    return x * ASCALE if f in (2, 3) else x


def given(f, x):
    return x * (1.0 / ASCALE) if f in (2, 3) else x


def run_main(fields, outs, scratch):
    state, wet = scratch[0], scratch[-1]

    def load_in(k, _):
        for f in range(4):
            state[f, k, 0:ROWS] = held(f, fields[f][k])
        wet[k, 0:ROWS] = fields[4][k].astype(jnp.float32)
        return 0

    lax.fori_loop(0, LEVELS, load_in, 0, unroll=True)
    turn_rows = coriolis(lax.broadcasted_iota(jnp.int32, (ROWS, LANES), 0))
    run_substeps(LEVELS, CHUNKS, pressure_by_level, turn_rows, *scratch)

    def store_out(k, _):
        for f in range(4):
            outs[f, k] = given(f, state[f, k, 0:ROWS])
        return 0

    lax.fori_loop(0, LEVELS, store_out, 0, unroll=True)


def run_bands(rim, halo, out, scratch):
    state, wet = scratch[0], scratch[-1]

    def load_in(k, _):
        for f in range(4):
            state[f, k, 0:8] = held(f, rim[f, k, 8:16])
            state[f, k, 8:16] = held(f, halo[f, k])
            state[f, k, 16:24] = held(f, rim[f, k, 0:8])
        wet[k, 0:8] = rim[4, k, 8:16]
        wet[k, 8:16] = halo[4, k]
        wet[k, 16:24] = rim[4, k, 0:8]
        return 0

    lax.fori_loop(0, LEVELS, load_in, 0, unroll=True)
    place = lax.broadcasted_iota(jnp.int32, (24, LANES), 0)
    turn_rows = coriolis(jnp.where(place < 12, place + (ROWS - 8), place - 16))
    run_substeps(LEVELS, 3, pressure_by_level, turn_rows, *scratch)

    def store_out(k, _):
        for f in range(4):
            out[f, k, 0:8] = given(f, state[f, k, 16:24])
            out[f, k, 8:16] = given(f, state[f, k, 0:8])
        return 0

    lax.fori_loop(0, LEVELS, store_out, 0, unroll=True)


MAIN = jax.ShapeDtypeStruct((4, LEVELS, ROWS, LANES), jnp.float32)


def first_body(*refs):
    fields, (out, edges, part_b, part_a, rim, to_a), scratch = refs[:5], refs[5:11], refs[11:]
    pack_columns(fields, edges, part_b, part_a, rim)
    start = pl.multiple_of(jnp.where(odd_lat(), 0, 8), 8)
    pack_pairs(lambda f, k: rim[f, k, pl.ds(start, 8)], jnp.logical_not(odd_lat()), to_a)

    @pl.when(main_slot() == 0)
    def _():
        run_main(fields, out, scratch)


def first_block(fields):
    f32 = jnp.float32
    part = jax.ShapeDtypeStruct((CHUNKS + CHUNKS // 4, 8, LANES), f32)
    return pl.pallas_call(
        first_body,
        out_shape=[
            MAIN,
            jax.ShapeDtypeStruct((5, ROWS, LANES), f32),
            part,
            part,
            jax.ShapeDtypeStruct((5, LEVELS, 16, LANES), f32),
            jax.ShapeDtypeStruct((5, LEVELS // 2, 8, LANES), f32),
        ],
        scratch_shapes=step_scratch(LEVELS, CHUNKS),
        compiler_params=pltpu.CompilerParams(vmem_limit_bytes=VMEM),
        cost_estimate=pl.CostEstimate(flops=300_000_000, bytes_accessed=20_000_000, transcendentals=0),
        name="first_block",
    )(*fields)


def second_body(*refs):
    fields, (out, done), scratch = refs[:5], refs[6:8], refs[8:]
    done[...] = jnp.zeros_like(done)

    @pl.when(main_slot() == 1)
    def _():
        run_main(fields, out, scratch)


def second_block(fields, after):
    return pl.pallas_call(
        second_body,
        out_shape=[MAIN, jax.ShapeDtypeStruct((8, LANES), jnp.float32)],
        scratch_shapes=step_scratch(LEVELS, CHUNKS),
        compiler_params=pltpu.CompilerParams(vmem_limit_bytes=VMEM),
        cost_estimate=pl.CostEstimate(flops=300_000_000, bytes_accessed=20_000_000, transcendentals=0),
        name="second_block",
    )(*fields, after)


def third_body(*refs):
    fields, (rim, halo, out, band) = refs[:5], refs[5:9]
    main_scratch, band_scratch = refs[9:19], refs[19:]

    @pl.when(main_slot() == 2)
    def _():
        run_main(fields, out, main_scratch)

    run_bands(rim, halo, band, band_scratch)


def third_block(fields, rim, halo):
    return pl.pallas_call(
        third_body,
        out_shape=[MAIN, jax.ShapeDtypeStruct((4, LEVELS, 16, LANES), jnp.float32)],
        scratch_shapes=step_scratch(LEVELS, CHUNKS) + step_scratch(LEVELS, 3),
        compiler_params=pltpu.CompilerParams(vmem_limit_bytes=VMEM),
        cost_estimate=pl.CostEstimate(flops=200_000_000, bytes_accessed=10_000_000, transcendentals=0),
        name="third_block",
    )(*fields, rim, halo)


TALL = CHUNKS + 2


def pressure_by_lanes(rows, src):
    group = lax.broadcasted_iota(jnp.int32, (rows, LANES), 1) // 16
    depth = (group.astype(jnp.float32) + 0.5) / LEVELS
    source = lax.broadcasted_iota(jnp.int32, (LANES, 2 * LANES), 0)
    target = lax.broadcasted_iota(jnp.int32, (LANES, 2 * LANES), 1)
    target = jnp.where(target < LANES, target, (target - (LANES - 1)) % LANES)
    same = (source % 16) == (target % 16)
    weights = jnp.where(same & (source < target), 2.0, jnp.where(source == target, 1.0, 0.0))
    both = jnp.concatenate([density_tenth(src[0, t, 0:rows], src[1, t, 0:rows], depth) for t in range(2)], axis=0)
    pieces = []
    for _ in range(3):
        pieces.append(both.astype(jnp.bfloat16))
        both = both - pieces[-1].astype(jnp.float32)
    p = jnp.dot(jnp.concatenate(pieces, axis=0), weights.astype(jnp.bfloat16), preferred_element_type=jnp.float32)
    p = (p[4 * rows :] + p[2 * rows : 4 * rows]) + p[: 2 * rows]
    yield p[:rows, :LANES], p[:rows, LANES:]
    yield p[rows:, :LANES], p[rows:, LANES:]


def strips_body(edges, edge_halo, from_b, from_a, band, *refs):
    mains, outs, scratch = refs[:3], refs[3:7], refs[7:17]
    merged, sent = refs[17:]
    slot_now = jnp.full((8, LANES), main_slot())
    state, wet = scratch[0], scratch[-1]
    odd = odd_lon()
    lane = lane_index()
    place = lane % 16
    east_halo = (place >= 8) & (place < 12)
    west_halo = (place >= 4) & (place < 8)
    for i in range(CHUNKS + 1):
        for f in range(5):
            slot, chunk = (f, i) if f < 4 else (i % 4, CHUNKS + 1 + i // 4)
            own = edges[f, 8 * i : 8 * i + 8] if i < CHUNKS else edge_halo[f]
            a, b = from_a[chunk], from_b[chunk]
            east = jnp.where(east_halo, lane_roll(jnp.where(odd, b, a), 8 - 4 * slot), own)
            west = jnp.where(west_halo, lane_roll(jnp.where(odd, a, b), 8 - 4 * slot), own)
            for c in [1 + i] if i < CHUNKS else [0, CHUNKS + 1]:
                for t, tile in enumerate((east, west)):
                    if f < 4:
                        state[f, t, 8 * c : 8 * c + 8] = held(f, tile)
                    else:
                        wet[t, 8 * c : 8 * c + 8] = tile

    turn_rows = coriolis(lax.broadcasted_iota(jnp.int32, (8 * TALL, LANES), 0) - 8)
    run_substeps(2, TALL, pressure_by_lanes, turn_rows, *scratch)

    upper = row_index() < 4
    outer = (lane < 4) | (lane >= LANES - 4)
    copies = []
    for f in range(4):
        for i in range(CHUNKS):
            rows = pl.ds(8 * i, 8)
            c = 8 * (i + 1)
            edge = given(f, jnp.where(place < 8, state[f, 0, c : c + 8], state[f, 1, c : c + 8]))
            for k in range(LEVELS):
                block = jnp.where(slot_now == 1, mains[1][f, k, rows], mains[2][f, k, rows])
                block = jnp.where(slot_now == 0, mains[0][f, k, rows], block)
                if i == 0:
                    block = jnp.where(upper, band[f, k, 0:8], block)
                if i == CHUNKS - 1:
                    block = jnp.where(upper, block, band[f, k, 8:16])
                merged[f, k, rows] = jnp.where(outer, lane_roll(edge, -(16 * k + 8)), block)
        for n in range(2):
            half = pl.ds(n * LEVELS // 2, LEVELS // 2)
            copies.append(pltpu.make_async_copy(merged.at[f, half], outs[f].at[half], sent.at[2 * f + n]))
            copies[-1].start()
    for copy in copies:
        copy.wait()


def strips_and_merge(edges, edge_halo, from_b, from_a, band, mains):
    out = jax.ShapeDtypeStruct((LEVELS, ROWS, LANES), jnp.float32)
    return pl.pallas_call(
        strips_body,
        out_specs=[pl.BlockSpec(memory_space=pl.ANY)] * 4,
        out_shape=[out] * 4,
        scratch_shapes=step_scratch(2, TALL)
        + [pltpu.VMEM((4, LEVELS, ROWS, LANES), jnp.float32), pltpu.SemaphoreType.DMA((8,))],
        compiler_params=pltpu.CompilerParams(vmem_limit_bytes=VMEM),
        name="strips_and_merge",
    )(edges, edge_halo, from_b, from_a, band, *mains)


def lat_routes(lats, lons):
    first, second = [], []
    for j in range(lons):
        for i in range(lats):
            first.append((i * lons + j, (i ^ 1) * lons + j))
        for i in range(1, lats - 1):
            other = i + 1 if i % 2 else i - 1
            second.append((i * lons + j, other * lons + j))
        second.append(((lats - 1) * lons + j, (lats - 1) * lons + lons - 1 - j))
    return first, second


def lon_routes(lons):
    first = [(j, j ^ 1) for j in range(lons)]
    second = [(j, (j + 1 if j % 2 else j - 1) % lons) for j in range(lons)]
    return first, second


def on_device(*args):
    route_a, route_b = lat_routes(lax.axis_size("lat"), lax.axis_size("lon"))
    from_b = lax.ppermute(pack_rows(args), AXES, route_b)
    main_0, edges, part_b, part_a, rim, to_a = first_block(args)
    from_a = lax.ppermute(to_a, AXES, route_a)
    main_1, done = second_block(args, edges)
    halo, edge_halo, to_b, to_a = assemble(from_b, from_a, part_b, part_a, done)
    route_a, route_b = lon_routes(lax.axis_size("lon"))
    from_b = lax.ppermute(to_b, "lon", route_b)
    from_a = lax.ppermute(to_a, "lon", route_a)
    main_2, band = third_block(args, rim, halo)
    return tuple(strips_and_merge(edges, edge_halo, from_b, from_a, band, (main_0, main_1, main_2)))


def solution(mesh):
    spec = P(None, "lat", "lon")
    return jax.shard_map(
        on_device,
        mesh=mesh,
        in_specs=(spec,) * 5,
        out_specs=(spec,) * 4,
        check_vma=False,
    )
```
